512 devices in a mesh: adapter: 64 (over z, x, core), tensor: 8 (over y).
Axes of the slice: x: 4, y: 8, z: 8, core: 2. Of those that a mesh axis runs over, the one named last changes fastest.
Arguments:
- tokens: bfloat16 [8192, 8192], P('adapter', 'tensor'), may hold values from -6 to 6
- token_adapter_index: int32 [8192, 1], P('adapter'), may hold values from 0 to 127; in each aligned block of 128 rows (0 to 127, 128 to 255, ...) at most 3 rows name the same one
- key_value_weight: bfloat16 [8192, 2, 1024], P('tensor'), may hold values from -0.0625 to 0.0625
- adapter_down_weight: bfloat16 [128, 8192, 128], P('adapter', 'tensor'), may hold values from -0.0625 to 0.0625
- adapter_up_query: bfloat16 [128, 64, 8192], P('adapter', None, 'tensor'), may hold values from -0.75 to 0.75
- adapter_up_value: bfloat16 [128, 64, 1024], P('adapter', None, 'tensor'), may hold values from -0.75 to 0.75
Outputs:
- q_delta: bfloat16 [8192, 8192], P('adapter', 'tensor')
- keys: bfloat16 [8192, 1024], P('adapter', 'tensor')
- values: bfloat16 [8192, 1024], P('adapter', 'tensor')
The draws below stay inside these ranges and needn't reach their ends.
Inputs may be any that keep to these rules, and one draw needn't show every extreme that they name: `token_adapter_index`: among the 128 tokens of one index of the adapter axis no adapter occurs more than 3 times.
All inputs are finite; a program needn't handle non-finite values.
Results may differ from the reference program's by a relative error of at most 0.0049.
Values may be sent and summed in bfloat16 or wider, within the bound.
A program may use at most 64 MiB of HBM per device.

```python
import math
import jax
import jax.numpy as jnp
import numpy as np
from jax import lax

MODEL_WIDTH = 8192
QUERY_WIDTH = 8192
KEY_VALUE_WIDTH = 1024
ADAPTER_RANK = 64
TOK_DEV = 128
ADAPTER_TOTAL = 128
MOST = 3
TOKENS = 8192


def block_scale(own_key, dims, shards, least, largest):
    gain, own = 1.0, jax.random.fold_in(own_key, 6)
    for axis_at, blocks in shards:
        steps = jnp.exp(jax.random.uniform(jax.random.fold_in(own, axis_at), (blocks,), jnp.float32, least / len(shards), largest / len(shards)))
        gain = gain * jnp.repeat(steps, dims[axis_at] // blocks).reshape([-1 if axis == axis_at else 1 for axis in range(len(dims))])
    return gain


def routed_block(stream_key, own, number, rows, number_of, top, limit, slope):
    sequence = jax.random.permutation(stream_key, number_of)
    packed, usual = shares(number_of, rows * top, limit, slope, True), shares(number_of, rows * top, limit, slope, False)
    places = jnp.arange(number_of)

    def named(lengths, offset_by):
        used = int((lengths > 0).sum())
        fixed = max(1, used // 4)
        shifted = fixed + (places - fixed + offset_by * (used - fixed)) % max(1, number_of - fixed)
        return jnp.zeros((number_of,), jnp.int32).at[sequence[jnp.where(places < fixed, places, shifted)]].set(jnp.asarray(lengths, jnp.int32))

    lengths = jnp.where(number % 4 == 0, named(packed, number // 4), named(usual, number - number // 4 - 1))
    mixed = jax.random.permutation(jax.random.fold_in(own, 3), number_of)
    source_of, receiver = mixed[0:number_of // 2 * 2:2], mixed[1:number_of // 2 * 2:2]
    margin = jnp.minimum(lengths[source_of] - 1, limit - lengths[receiver]) // 2
    margin = jnp.where((source_of == sequence[0]) | (receiver == sequence[0]) | (lengths[receiver] == 0), 0, jnp.maximum(margin, 0))
    shifted = jax.random.randint(jax.random.fold_in(own, 4), (number_of // 2,), 0, 1 << 20) % (margin + 1)
    lengths = lengths.at[source_of].add(-shifted).at[receiver].add(shifted)
    items = jnp.searchsorted(jnp.cumsum(lengths), jnp.arange(rows * top), side="right").astype(jnp.int32)
    listing = items.reshape(top, rows).T
    listing = listing[jax.random.permutation(jax.random.fold_in(own, 1), rows)]
    offset_by = jax.random.randint(jax.random.fold_in(own, 2), (rows, 1), 0, top)
    return jnp.take_along_axis(listing, (jnp.arange(top)[None, :] + offset_by) % top, axis=1)


def shares(count, total, most, slope, full):
    loads = [(1 << 20) // math.isqrt(standing ** slope) + 1 for standing in range(1, count + 1)]
    largest = most if full else min(most, max(-(-total // count), total * loads[0] // sum(loads)))
    least = 1 if total - largest >= count - 1 else 0
    given, rest = [largest] + [least] * (count - 1), total - largest - least * (count - 1)
    while rest > 0:
        movable = [i for i in range(1, count) if given[i] < largest] or [i for i in range(1, count) if given[i] < most]
        whole, remaining = sum([loads[i] for i in movable]), rest
        for i in movable:
            extra = min(most - given[i], max(1, remaining * loads[i] // whole), rest)
            given[i] = given[i] + extra
            rest = rest - extra
    return np.array(given)


def gaussian(rng, extent, spread, limit, pieces=(), kind=jnp.bfloat16):
    drawn = spread * jax.random.normal(rng, extent, jnp.float32)
    if pieces:
        drawn = drawn * block_scale(rng, extent, pieces, -0.22, 0.18)
    return jnp.clip(drawn, -limit, limit).astype(kind)


def setup_inputs(seed: int = 0) -> dict:
    seeds = jax.random.split(jax.random.key(seed), 7)
    tokens = gaussian(seeds[0], (TOKENS, MODEL_WIDTH), 1.0, 6.0, ((0, 64), (1, 8)))
    token_adapter_index_keys = jax.random.split(jax.random.fold_in(seeds[1], 1), TOKENS // TOK_DEV)
    token_adapter_index_turns = jax.random.permutation(jax.random.fold_in(seeds[1], 3), TOKENS // TOK_DEV)
    token_adapter_index = jax.vmap(lambda own, number: routed_block(jax.random.fold_in(seeds[1], 2), own, number, TOK_DEV, ADAPTER_TOTAL, 1, MOST, 2))(token_adapter_index_keys, token_adapter_index_turns).reshape((TOKENS, 1))
    key_value_weight = gaussian(seeds[2], (MODEL_WIDTH, 2, KEY_VALUE_WIDTH), MODEL_WIDTH ** -0.5, 0.0625, ((0, 8),))
    adapter_down_weight = gaussian(seeds[3], (ADAPTER_TOTAL, MODEL_WIDTH, 2 * ADAPTER_RANK), MODEL_WIDTH ** -0.5, 0.0625, ((0, 64), (1, 8)))
    adapter_up_query = gaussian(seeds[4], (ADAPTER_TOTAL, ADAPTER_RANK, QUERY_WIDTH), ADAPTER_RANK ** -0.5, 0.75, ((0, 64), (2, 8)))
    adapter_up_value = gaussian(seeds[5], (ADAPTER_TOTAL, ADAPTER_RANK, KEY_VALUE_WIDTH), ADAPTER_RANK ** -0.5, 0.75, ((0, 64), (2, 8)))
    return {"tokens": tokens, "token_adapter_index": token_adapter_index, "key_value_weight": key_value_weight, "adapter_down_weight": adapter_down_weight, "adapter_up_query": adapter_up_query, "adapter_up_value": adapter_up_value}


def reference(tokens, token_adapter_index, key_value_weight, adapter_down_weight, adapter_up_query, adapter_up_value):
    adapter_of = token_adapter_index[:, 0]
    block_rows = min(32, TOKENS)
    block_count = TOKENS // block_rows

    def one_block(index):
        start = index * block_rows
        rows = lax.dynamic_slice_in_dim(tokens, start, block_rows, 0).astype(jnp.float32)
        selected_adapter = lax.dynamic_slice_in_dim(adapter_of, start, block_rows, 0)
        down_weight = jnp.take(adapter_down_weight, selected_adapter, axis=0).astype(jnp.float32)
        reduced_hidden = jnp.einsum("bd,bdr->br", rows, down_weight).astype(jnp.bfloat16)
        reduced_hidden = lax.optimization_barrier(reduced_hidden).astype(jnp.float32)
        query_up_weight = jnp.take(adapter_up_query, selected_adapter, axis=0).astype(jnp.float32)
        value_up_weight = jnp.take(adapter_up_value, selected_adapter, axis=0).astype(jnp.float32)
        delta_q = jnp.einsum("br,brq->bq", reduced_hidden[:, :ADAPTER_RANK], query_up_weight)
        delta_v = jnp.einsum("br,brq->bq", reduced_hidden[:, ADAPTER_RANK:], value_up_weight)
        return delta_q.astype(jnp.bfloat16), delta_v.astype(jnp.bfloat16)

    delta_q, delta_v = lax.map(one_block, jnp.arange(block_count, dtype=jnp.int32))
    q_delta = delta_q.reshape(TOKENS, QUERY_WIDTH)
    v_delta = delta_v.reshape(TOKENS, KEY_VALUE_WIDTH)
    base = jnp.dot(tokens, key_value_weight.reshape(MODEL_WIDTH, 2 * KEY_VALUE_WIDTH), preferred_element_type=jnp.float32)
    base = base.reshape(TOKENS, 2, KEY_VALUE_WIDTH)
    keys = base[:, 0, :].astype(jnp.bfloat16)
    values = (base[:, 1, :] + v_delta.astype(jnp.float32)).astype(jnp.bfloat16)
    return (q_delta, keys, values)
```

```python
import functools
import jax
import jax.numpy as jnp
from jax import lax
from jax.experimental import pallas as pl
from jax.experimental.pallas import tpu as pltpu
from jax.sharding import PartitionSpec as P

MESH = pl.DeviceIdType.MESH
LANES = 128
BF16 = jnp.bfloat16
F32 = jnp.float32
MOST = 3
ZS, XS, CORES = 8, 4, 2
CHUNKS = 2


def kernel(
    holders,
    tensors,
    tok_hbm,
    idx_hbm,
    kvw_hbm,
    down_hbm,
    upq_hbm,
    upv_hbm,
    q_out,
    k_out,
    v_out,
    tok,
    idx,
    kvw,
    wbase,
    lhs,
    down,
    up,
    fsel,
    stage,
    send,
    recv,
    xs,
    part,
    rs,
    sh,
    ustage,
    ret_send,
    ret_recv,
    bs_send,
    bs_recv,
    load_sems,
    send_sems,
    recv_sems,
):
    me = lax.axis_index("adapter")
    t = lax.axis_index("tensor")
    rows, features = tok.shape
    blocks = features // LANES
    per_holder = down.shape[0]
    adapters = holders * per_holder
    tile = per_holder * blocks
    chunk = holders // CHUNKS
    z = me // (XS * CORES)
    x = (me // CORES) % XS
    core = me % CORES
    self_pos = z * CORES + core

    def peer_of(p):
        near = (p // (ZS * CORES)) % 2
        far = p // (2 * ZS * CORES)
        px = (x + near * (1 - 2 * (x % 2)) + 2 * far) % XS
        return ((p // CORES) % ZS) * (XS * CORES) + px * CORES + p % CORES

    def my_pos(p):
        return (p // (ZS * CORES)) * (ZS * CORES) + self_pos

    def position(k, d):
        return k * chunk + (self_pos + d) % chunk

    def for_peers(k, act):
        @pl.loop(1 if k == 0 else 0, chunk)
        def _(d):
            act(position(k, d))

    barrier = pltpu.get_barrier_semaphore()

    @pl.loop(1, tensors)
    def _(d):
        pl.semaphore_signal(barrier, inc=1, device_id=(me, (t + d) % tensors), device_id_type=MESH)

    @pl.loop(1, holders)
    def _(d):
        pl.semaphore_signal(barrier, inc=1, device_id=((me + d) % holders, t), device_id_type=MESH)

    get_tok = pltpu.make_async_copy(tok_hbm, tok, load_sems.at[0])
    get_idx = pltpu.make_async_copy(idx_hbm, idx, load_sems.at[1])
    get_kvw = pltpu.make_async_copy(kvw_hbm, kvw, load_sems.at[2])
    get_down = pltpu.make_async_copy(down_hbm, down, load_sems.at[3])
    get_idx.start()
    get_tok.start()
    get_kvw.start()
    get_down.start()

    get_idx.wait()
    lane = lax.broadcasted_iota(jnp.int32, (rows, adapters), 1)
    picked = (idx[...] == lane).astype(F32)
    earlier = lax.broadcasted_iota(jnp.int32, (rows, rows), 0) > lax.broadcasted_iota(
        jnp.int32, (rows, rows), 1
    )
    ordinal = jnp.dot(
        earlier.astype(F32).astype(BF16), picked.astype(BF16), preferred_element_type=F32
    )
    get_tok.wait()
    for m in range(MOST):
        chosen = jnp.where(ordinal == float(m), picked, 0.0)
        fsel[:, m * adapters : (m + 1) * adapters] = chosen.astype(BF16)
        gathered = jnp.dot(chosen.T.astype(BF16), tok[...], preferred_element_type=F32)
        for j in range(blocks):
            stage[m, pl.ds(j, adapters, stride=blocks), :] = gathered[:, j * LANES : (j + 1) * LANES]
        send[:, :, m * LANES : (m + 1) * LANES] = (
            stage[m].reshape(holders, tile, LANES).astype(BF16)
        )

    pl.semaphore_wait(barrier, tensors - 1 + holders - 1)

    def dispatch(k, p):
        return pltpu.make_async_remote_copy(
            src_ref=send.at[peer_of(p)],
            dst_ref=recv.at[my_pos(p)],
            send_sem=send_sems.at[0],
            recv_sem=recv_sems.at[k],
            device_id=(peer_of(p), t),
            device_id_type=MESH,
        )

    for k in range(CHUNKS):
        for_peers(k, lambda p, k=k: dispatch(k, p).start())
    recv[self_pos] = send[me]

    up[...] = jnp.zeros_like(up)
    get_ups = []
    for a in range(per_holder):
        rank = upq_hbm.shape[1]
        get_ups.append(
            pltpu.make_async_copy(
                upq_hbm.at[a], up.at[a, pl.ds(0, rank), pl.ds(0, features)], load_sems.at[4 + a]
            )
        )
        get_ups.append(
            pltpu.make_async_copy(
                upv_hbm.at[a],
                up.at[a, pl.ds(rank, rank), pl.ds(features, LANES)],
                load_sems.at[4 + per_holder + a],
            )
        )
    for copy in get_ups:
        copy.start()
    for c in range(2):
        spread = (
            lax.broadcasted_iota(jnp.int32, (LANES, 2 * LANES), 1)
            == 2 * lax.broadcasted_iota(jnp.int32, (LANES, 2 * LANES), 0) + c
        ).astype(F32).astype(BF16)
        for j in range(blocks):
            lhs[c, :, 2 * j * LANES : 2 * (j + 1) * LANES] = jnp.dot(
                tok[:, j * LANES : (j + 1) * LANES], spread, preferred_element_type=F32
            ).astype(BF16)
    get_kvw.wait()
    step = 32

    @pl.loop(0, features // step)
    def _(i):
        wbase[pl.ds(i * 2 * step, 2 * step), :] = kvw[pl.ds(i * step, step)].reshape(
            2 * step, wbase.shape[1]
        )

    @pl.loop(0, tensors // 2)
    def _(n):
        columns = pl.ds(pl.multiple_of(n * 2 * LANES, 2 * LANES), 2 * LANES)
        for c in range(2):
            terms = jnp.dot(lhs[c], wbase[:, columns], preferred_element_type=F32).astype(BF16)
            for half in range(2):
                bs_send[2 * n + half, :, c * LANES : (c + 1) * LANES] = terms[
                    :, half * LANES : (half + 1) * LANES
                ]

    def base_copy(d):
        other = (t + d) % tensors
        return pltpu.make_async_remote_copy(
            src_ref=bs_send.at[other],
            dst_ref=bs_recv.at[t],
            send_sem=send_sems.at[1],
            recv_sem=recv_sems.at[2],
            device_id=(me, other),
            device_id_type=MESH,
        )

    @pl.loop(1, tensors)
    def _(d):
        base_copy(d).start()

    bs_recv[t] = bs_send[t]
    ustage[MOST] = jnp.zeros_like(ustage[MOST])

    share = MOST * per_holder * chunk // tensors

    def partial(k):
        for m in range(MOST):
            stage[m, pl.ds(0, chunk * tile), :] = (
                recv[pl.ds(k * chunk, chunk), :, m * LANES : (m + 1) * LANES]
                .astype(F32)
                .reshape(chunk * tile, LANES)
            )
        for a in range(per_holder):
            for m in range(MOST):
                for j in range(blocks):
                    xs[a, m * chunk : (m + 1) * chunk, j * LANES : (j + 1) * LANES] = stage[
                        m, pl.ds(a * blocks + j, chunk, stride=tile), :
                    ].astype(BF16)
            terms = jnp.dot(xs[a], down[a], preferred_element_type=F32)
            owners = tensors // per_holder
            for s in range(owners):
                part[k, a * owners + s] = terms[s * share : (s + 1) * share]

        def scatter(d):
            other = (t + d) % tensors
            return pltpu.make_async_remote_copy(
                src_ref=part.at[k, other],
                dst_ref=rs.at[k, t],
                send_sem=send_sems.at[2],
                recv_sem=recv_sems.at[3 + k],
                device_id=(me, other),
                device_id_type=MESH,
            )

        @pl.loop(1, tensors)
        def _(d):
            scatter(d).start()

        rs[k, t] = part[k, t]

    def wait_bytes(ref, sem):
        pltpu.make_async_copy(ref, ref, sem).wait()

    def total(k):
        wait_bytes(rs.at[k, pl.ds(0, tensors - 1)], recv_sems.at[3 + k])
        summed = rs[k, 0]
        for s in range(1, tensors):
            summed = summed + rs[k, s]
        padded = jnp.concatenate([summed, jnp.zeros((sh.shape[2] - share, LANES), F32)], axis=0)
        sh[k, t] = padded.astype(BF16)

        def gather(d):
            return pltpu.make_async_remote_copy(
                src_ref=sh.at[k, t],
                dst_ref=sh.at[k, t],
                send_sem=send_sems.at[3],
                recv_sem=recv_sems.at[5 + k],
                device_id=(me, (t + d) % tensors),
                device_id_type=MESH,
            )

        @pl.loop(1, tensors)
        def _(d):
            gather(d).start()

    def corrections(k):
        wait_bytes(sh.at[k, pl.ds(0, tensors - 1)], recv_sems.at[5 + k])
        shrunk = sh[k].astype(F32)[:, :share].reshape(tensors * share, LANES).astype(BF16)
        each = MOST * chunk
        for a in range(per_holder):
            deltas = jnp.dot(
                shrunk[a * each : (a + 1) * each], up[a], preferred_element_type=F32
            )
            for m in range(MOST):
                of_m = deltas[m * chunk : (m + 1) * chunk]
                for j in range(blocks):
                    ustage[m, pl.ds(a * blocks + j, chunk, stride=tile), :] = of_m[
                        :, j * LANES : (j + 1) * LANES
                    ]
                ustage[MOST, pl.ds(a * blocks + m, chunk, stride=tile), :] = of_m[:, features:]
        for m in range(MOST + 1):
            ret_send[pl.ds(k * chunk, chunk), :, m * LANES : (m + 1) * LANES] = (
                ustage[m].reshape(chunk, tile, LANES).astype(BF16)
            )

        def give_back(p):
            return pltpu.make_async_remote_copy(
                src_ref=ret_send.at[p],
                dst_ref=ret_recv.at[me],
                send_sem=send_sems.at[4],
                recv_sem=recv_sems.at[7],
                device_id=(peer_of(p), t),
                device_id_type=MESH,
            )

        for_peers(k, lambda p: give_back(p).start())
        if k == 0:
            ret_recv[me] = ret_send[self_pos]

    get_down.wait()
    for copy in get_ups:
        copy.wait()
    for k in range(CHUNKS):
        arrivals = chunk - 1 if k == 0 else chunk
        wait_bytes(recv.at[pl.ds(0, arrivals)], recv_sems.at[k])
        partial(k)
        total(k)
        corrections(k)

    wait_bytes(bs_recv.at[pl.ds(0, tensors - 1)], recv_sems.at[2])
    base = bs_recv[0].astype(F32)
    for s in range(1, tensors):
        base = base + bs_recv[s].astype(F32)
    k_out[...] = base[:, :LANES].astype(BF16)

    wait_bytes(ret_recv.at[pl.ds(0, holders - 1)], recv_sems.at[7])
    for m in range(MOST + 1):
        stage[m] = (
            ret_recv[:, :, m * LANES : (m + 1) * LANES].astype(F32).reshape(holders * tile, LANES)
        )

    def picked_rows(refs):
        gathered = jnp.concatenate(
            [stage[m, pl.ds(start, adapters, stride=blocks), :] for m, start in refs], axis=0
        ).astype(BF16)
        return jnp.dot(fsel[...], gathered, preferred_element_type=F32)

    for j in range(blocks):
        q_out[:, j * LANES : (j + 1) * LANES] = picked_rows([(m, j) for m in range(MOST)]).astype(
            BF16
        )
    v_out[...] = (base[:, LANES:] + picked_rows([(MOST, m) for m in range(MOST)])).astype(BF16)

    wait_bytes(send.at[pl.ds(0, holders - 1)], send_sems.at[0])
    wait_bytes(bs_send.at[pl.ds(0, tensors - 1)], send_sems.at[1])
    for k in range(CHUNKS):
        wait_bytes(part.at[k, pl.ds(0, tensors - 1)], send_sems.at[2])
        wait_bytes(sh.at[k, pl.ds(0, tensors - 1)], send_sems.at[3])
    wait_bytes(ret_send.at[pl.ds(0, holders - 1)], send_sems.at[4])


def local(holders, tensors, tokens, index, kv_weight, down, up_query, up_value):
    rows, features = tokens.shape
    head = kv_weight.shape[2] // tensors
    per_holder = down.shape[0]
    blocks = features // LANES
    tile = per_holder * blocks
    chunk = holders // CHUNKS
    share = MOST * per_holder * chunk // tensors
    vmem = pltpu.VMEM
    dma = pltpu.SemaphoreType.DMA
    scratch = [
        vmem(tokens.shape, BF16),
        vmem(index.shape, jnp.int32),
        vmem(kv_weight.shape, BF16),
        vmem((2 * features, kv_weight.shape[2]), BF16),
        vmem((2, rows, 2 * features), BF16),
        vmem(down.shape, BF16),
        vmem((per_holder, 2 * up_query.shape[1], features + LANES), BF16),
        vmem((rows, MOST * holders * per_holder), BF16),
        vmem((MOST + 1, holders * tile, LANES), F32),
        vmem((holders, tile, MOST * LANES), BF16),
        vmem((holders, tile, MOST * LANES), BF16),
        vmem((per_holder, MOST * chunk, features), BF16),
        vmem((CHUNKS, tensors, share, LANES), F32),
        vmem((CHUNKS, tensors, share, LANES), F32),
        vmem((CHUNKS, tensors, -(-share // 16) * 16, LANES), BF16),
        vmem((MOST + 1, chunk * tile, LANES), F32),
        vmem((holders, tile, (MOST + 1) * LANES), BF16),
        vmem((holders, tile, (MOST + 1) * LANES), BF16),
        vmem((tensors, rows, 2 * head), BF16),
        vmem((tensors, rows, 2 * head), BF16),
        dma((4 + 2 * per_holder,)),
        dma((5,)),
        dma((8,)),
    ]
    return pl.pallas_call(
        functools.partial(kernel, holders, tensors),
        out_shape=(
            jax.ShapeDtypeStruct((rows, features), BF16),
            jax.ShapeDtypeStruct((rows, head), BF16),
            jax.ShapeDtypeStruct((rows, head), BF16),
        ),
        in_specs=[pl.BlockSpec(memory_space=pl.ANY)] * 6,
        out_specs=tuple([pl.BlockSpec(memory_space=vmem)] * 3),
        scratch_shapes=scratch,
        compiler_params=pltpu.CompilerParams(
            collective_id=0, has_side_effects=True, vmem_limit_bytes=56 << 20
        ),
        name="adapters",
    )(tokens, index, kv_weight, down, up_query, up_value)


def solution(mesh):
    placed = (
        P("adapter", "tensor"),
        P("adapter", None),
        P("tensor", None, None),
        P("adapter", "tensor", None),
        P("adapter", None, "tensor"),
        P("adapter", None, "tensor"),
    )
    return jax.shard_map(
        functools.partial(local, mesh.shape["adapter"], mesh.shape["tensor"]),
        mesh=mesh,
        in_specs=placed,
        out_specs=(P("adapter", "tensor"), P("adapter", "tensor"), P("adapter", "tensor")),
        check_vma=False,
    )
```

```python
import functools
import jax
import jax.numpy as jnp
from jax import lax
from jax.experimental import pallas as pl
from jax.experimental.pallas import tpu as pltpu
from jax.sharding import PartitionSpec as P

MESH = pl.DeviceIdType.MESH
LANES = 128
BF16 = jnp.bfloat16
F32 = jnp.float32
MOST = 3
ZS, XS, CORES = 8, 4, 2
CHUNKS = 4


def kernel(
    holders,
    tensors,
    tok_hbm,
    idx_hbm,
    kvw_hbm,
    down_hbm,
    upq_hbm,
    upv_hbm,
    q_out,
    k_out,
    v_out,
    tok,
    idx,
    kvw,
    wbase,
    lhs,
    down,
    up,
    fsel,
    stage,
    send,
    recv,
    xs,
    part,
    rs,
    sh,
    ustage,
    ret_send,
    ret_recv,
    bs_send,
    bs_recv,
    load_sems,
    send_sems,
    recv_sems,
):
    me = lax.axis_index("adapter")
    t = lax.axis_index("tensor")
    rows, features = tok.shape
    blocks = features // LANES
    per_holder = down.shape[0]
    adapters = holders * per_holder
    tile = per_holder * blocks
    chunk = holders // CHUNKS
    z = me // (XS * CORES)
    x = (me // CORES) % XS
    core = me % CORES
    self_pos = z * CORES + core

    def peer_of(p):
        offset = p // chunk
        px = (x + offset % 2 * (1 - 2 * (x % 2)) + 2 * (offset // 2)) % XS
        return ((p // CORES) % ZS) * (XS * CORES) + px * CORES + p % CORES

    def my_pos(p):
        return (p // chunk) * chunk + self_pos

    def position(k, d):
        return k * chunk + (self_pos + d) % chunk

    def for_peers(k, act):
        @pl.loop(1 if k == 0 else 0, chunk)
        def _(d):
            act(position(k, d))

    get_tok = pltpu.make_async_copy(tok_hbm, tok, load_sems.at[0])
    get_idx = pltpu.make_async_copy(idx_hbm, idx, load_sems.at[1])
    get_kvw = pltpu.make_async_copy(kvw_hbm, kvw, load_sems.at[2])
    get_down = pltpu.make_async_copy(down_hbm, down, load_sems.at[3])
    get_idx.start()
    get_tok.start()

    barrier = pltpu.get_barrier_semaphore()

    @pl.loop(1, tensors)
    def _(d):
        pl.semaphore_signal(barrier, inc=1, device_id=(me, (t + d) % tensors), device_id_type=MESH)

    @pl.loop(1, holders)
    def _(d):
        pl.semaphore_signal(barrier, inc=1, device_id=((me + d) % holders, t), device_id_type=MESH)

    get_down.start()
    get_kvw.start()

    get_idx.wait()
    picked = (lax.broadcasted_iota(jnp.int32, (adapters, rows), 0) == idx[...]).astype(F32)
    earlier = lax.broadcasted_iota(jnp.int32, (rows, rows), 0) < lax.broadcasted_iota(
        jnp.int32, (rows, rows), 1
    )
    ordinal = jnp.dot(
        picked.astype(BF16), earlier.astype(F32).astype(BF16), preferred_element_type=F32
    )
    get_tok.wait()
    for m in range(MOST):
        chosen = jnp.where(ordinal == float(m), picked, 0.0)
        fsel[m * adapters : (m + 1) * adapters, :] = chosen
        gathered = jnp.dot(chosen.astype(BF16), tok[...], preferred_element_type=F32)
        for j in range(blocks):
            stage[m, pl.ds(j, adapters, stride=blocks), :] = gathered[:, j * LANES : (j + 1) * LANES]
        send[:, :, m * LANES : (m + 1) * LANES] = (
            stage[m].reshape(holders, tile, LANES).astype(BF16)
        )

    pl.semaphore_wait(barrier, tensors - 1 + holders - 1)

    def dispatch(k, p):
        return pltpu.make_async_remote_copy(
            src_ref=send.at[peer_of(p)],
            dst_ref=recv.at[my_pos(p)],
            send_sem=send_sems.at[0],
            recv_sem=recv_sems.at[3 + 2 * CHUNKS + k],
            device_id=(peer_of(p), t),
            device_id_type=MESH,
        )

    def dispatch_chunk(k):
        for_peers(k, lambda p: dispatch(k, p).start())

    dispatch_chunk(0)
    dispatch_chunk(1)
    recv[self_pos] = send[me]

    up[...] = jnp.zeros_like(up)
    get_ups = []
    for a in range(per_holder):
        rank = upq_hbm.shape[1]
        get_ups.append(
            pltpu.make_async_copy(
                upq_hbm.at[a], up.at[a, pl.ds(0, rank), pl.ds(0, features)], load_sems.at[4 + a]
            )
        )
        get_ups.append(
            pltpu.make_async_copy(
                upv_hbm.at[a],
                up.at[a, pl.ds(rank, rank), pl.ds(features, LANES)],
                load_sems.at[4 + per_holder + a],
            )
        )
    for copy in get_ups:
        copy.start()
    for c in range(2):
        spread = (
            lax.broadcasted_iota(jnp.int32, (LANES, 2 * LANES), 1)
            == 2 * lax.broadcasted_iota(jnp.int32, (LANES, 2 * LANES), 0) + c
        ).astype(F32).astype(BF16)
        for j in range(blocks):
            lhs[c, :, 2 * j * LANES : 2 * (j + 1) * LANES] = jnp.dot(
                tok[:, j * LANES : (j + 1) * LANES], spread, preferred_element_type=F32
            ).astype(BF16)
    dispatch_chunk(2)
    get_kvw.wait()
    run = 32

    @pl.loop(0, features // run)
    def _(i):
        wbase[pl.ds(i * 2 * run, 2 * run), :] = kvw[pl.ds(i * run, run)].reshape(
            2 * run, wbase.shape[1]
        )

    @pl.loop(0, tensors // 2)
    def _(n):
        columns = pl.ds(pl.multiple_of(n * 2 * LANES, 2 * LANES), 2 * LANES)
        for c in range(2):
            terms = jnp.dot(lhs[c], wbase[:, columns], preferred_element_type=F32).astype(BF16)
            for half in range(2):
                bs_send[2 * n + half, :, c * LANES : (c + 1) * LANES] = terms[
                    :, half * LANES : (half + 1) * LANES
                ]

    dispatch_chunk(3)
    def base_copy(d):
        other = (t + d) % tensors
        return pltpu.make_async_remote_copy(
            src_ref=bs_send.at[other],
            dst_ref=bs_recv.at[t],
            send_sem=send_sems.at[1],
            recv_sem=recv_sems.at[2],
            device_id=(me, other),
            device_id_type=MESH,
        )

    bs_recv[t] = bs_send[t]
    ustage[MOST] = jnp.zeros_like(ustage[MOST])

    owners = MOST * per_holder

    def wait_bytes(ref, sem):
        pltpu.make_async_copy(ref, ref, sem).wait()

    def partial(k):
        for m in range(MOST):
            stage[m, pl.ds(0, chunk * tile), :] = (
                recv[pl.ds(k * chunk, chunk), :, m * LANES : (m + 1) * LANES]
                .astype(F32)
                .reshape(chunk * tile, LANES)
            )
        for a in range(per_holder):
            for m in range(MOST):
                for j in range(blocks):
                    xs[a, m * chunk : (m + 1) * chunk, j * LANES : (j + 1) * LANES] = stage[
                        m, pl.ds(a * blocks + j, chunk, stride=tile), :
                    ].astype(BF16)
            terms = jnp.dot(xs[a], down[a], preferred_element_type=F32)
            for m in range(MOST):
                part[k, a * MOST + m] = terms[m * chunk : (m + 1) * chunk]

        @pl.loop(1, tensors)
        def _(d):
            other = (t + d) % tensors

            @pl.when(other < owners)
            def _():
                pltpu.make_async_remote_copy(
                    src_ref=part.at[k, other],
                    dst_ref=rs.at[k, t],
                    send_sem=send_sems.at[2],
                    recv_sem=recv_sems.at[3 + k],
                    device_id=(me, other),
                    device_id_type=MESH,
                ).start()

    def total(k):
        @pl.when(t < owners)
        def _():
            rs[k, t] = part[k, t]
            wait_bytes(rs.at[k, pl.ds(0, tensors - 1)], recv_sems.at[3 + k])
            summed = rs[k, 0]
            for s in range(1, tensors):
                summed = summed + rs[k, s]
            sh[k, t] = summed.astype(BF16)

            @pl.loop(1, tensors)
            def _(d):
                pltpu.make_async_remote_copy(
                    src_ref=sh.at[k, t],
                    dst_ref=sh.at[k, t],
                    send_sem=send_sems.at[3],
                    recv_sem=recv_sems.at[3 + CHUNKS + k],
                    device_id=(me, (t + d) % tensors),
                    device_id_type=MESH,
                ).start()

    def corrections(k):
        @pl.when(t < owners)
        def _():
            wait_bytes(sh.at[k, pl.ds(0, owners - 1)], recv_sems.at[3 + CHUNKS + k])

        @pl.when(t >= owners)
        def _():
            wait_bytes(sh.at[k, pl.ds(0, owners)], recv_sems.at[3 + CHUNKS + k])

        for a in range(per_holder):
            shrunk = sh[k, a * MOST : (a + 1) * MOST].reshape(MOST * chunk, LANES)
            deltas = jnp.dot(shrunk, up[a], preferred_element_type=F32)
            for m in range(MOST):
                of_m = deltas[m * chunk : (m + 1) * chunk]
                for j in range(blocks):
                    ustage[m, pl.ds(a * blocks + j, chunk, stride=tile), :] = of_m[
                        :, j * LANES : (j + 1) * LANES
                    ]
                ustage[MOST, pl.ds(a * blocks + m, chunk, stride=tile), :] = of_m[:, features:]
        for m in range(MOST + 1):
            ret_send[pl.ds(k * chunk, chunk), :, m * LANES : (m + 1) * LANES] = (
                ustage[m].reshape(chunk, tile, LANES).astype(BF16)
            )

        def give_back(p):
            return pltpu.make_async_remote_copy(
                src_ref=ret_send.at[p],
                dst_ref=ret_recv.at[me],
                send_sem=send_sems.at[4],
                recv_sem=recv_sems.at[0],
                device_id=(peer_of(p), t),
                device_id_type=MESH,
            )

        for_peers(k, lambda p: give_back(p).start())
        if k == 0:
            ret_recv[me] = ret_send[self_pos]

    def arrive(k):
        arrivals = chunk - 1 if k == 0 else chunk
        wait_bytes(recv.at[pl.ds(0, arrivals)], recv_sems.at[3 + 2 * CHUNKS + k])
        partial(k)

    def base_sends():
        @pl.loop(1, tensors)
        def _(d):
            base_copy(d).start()

    get_down.wait()
    for copy in get_ups:
        copy.wait()
    steps = ("a0", "a1", "b0", "a2", "b1", "c0", "a3", "b2", "c1", "b3", "base", "c2", "c3")
    for name in steps:
        if name == "base":
            base_sends()
        elif name[0] == "a":
            arrive(int(name[1]))
        elif name[0] == "b":
            total(int(name[1]))
        else:
            corrections(int(name[1]))

    wait_bytes(bs_recv.at[pl.ds(0, tensors - 1)], recv_sems.at[2])
    base = bs_recv[0].astype(F32)
    for s in range(1, tensors):
        base = base + bs_recv[s].astype(F32)
    k_out[...] = base[:, :LANES].astype(BF16)

    wait_bytes(ret_recv.at[pl.ds(0, holders - 1)], recv_sems.at[0])
    for m in range(MOST + 1):
        stage[m] = (
            ret_recv[:, :, m * LANES : (m + 1) * LANES].astype(F32).reshape(holders * tile, LANES)
        )

    chosen_rows = fsel[...].T.astype(BF16)

    def picked_rows(refs):
        gathered = jnp.concatenate(
            [stage[m, pl.ds(start, adapters, stride=blocks), :] for m, start in refs], axis=0
        ).astype(BF16)
        return jnp.dot(chosen_rows, gathered, preferred_element_type=F32)

    for j in range(blocks):
        q_out[:, j * LANES : (j + 1) * LANES] = picked_rows([(m, j) for m in range(MOST)]).astype(
            BF16
        )
    v_out[...] = (base[:, LANES:] + picked_rows([(MOST, m) for m in range(MOST)])).astype(BF16)

    wait_bytes(send.at[pl.ds(0, holders - 1)], send_sems.at[0])
    wait_bytes(bs_send.at[pl.ds(0, tensors - 1)], send_sems.at[1])

    @pl.when(t < owners)
    def _():
        for k in range(CHUNKS):
            wait_bytes(part.at[k, pl.ds(0, owners - 1)], send_sems.at[2])
            wait_bytes(rs.at[k, pl.ds(0, tensors - 1), pl.ds(0, chunk // 2)], send_sems.at[3])

    @pl.when(t >= owners)
    def _():
        for k in range(CHUNKS):
            wait_bytes(part.at[k, pl.ds(0, owners)], send_sems.at[2])

    wait_bytes(ret_send.at[pl.ds(0, holders - 1)], send_sems.at[4])


def step(holders, tensors, tokens, index, kv_weight, down, up_query, up_value):
    rows, features = tokens.shape
    head = kv_weight.shape[2] // tensors
    per_holder = down.shape[0]
    blocks = features // LANES
    tile = per_holder * blocks
    chunk = holders // CHUNKS
    owners = MOST * per_holder
    vmem = pltpu.VMEM
    dma = pltpu.SemaphoreType.DMA
    scratch = [
        vmem(tokens.shape, BF16),
        vmem((1, rows), jnp.int32),
        vmem(kv_weight.shape, BF16),
        vmem((2 * features, kv_weight.shape[2]), BF16),
        vmem((2, rows, 2 * features), BF16),
        vmem(down.shape, BF16),
        vmem((per_holder, 2 * up_query.shape[1], features + LANES), BF16),
        vmem((MOST * holders * per_holder, rows), F32),
        vmem((MOST + 1, holders * tile, LANES), F32),
        vmem((holders, tile, MOST * LANES), BF16),
        vmem((holders, tile, MOST * LANES), BF16),
        vmem((per_holder, MOST * chunk, features), BF16),
        vmem((CHUNKS, owners, chunk, LANES), F32),
        vmem((CHUNKS, tensors, chunk, LANES), F32),
        vmem((CHUNKS, owners, chunk, LANES), BF16),
        vmem((MOST + 1, chunk * tile, LANES), F32),
        vmem((holders, tile, (MOST + 1) * LANES), BF16),
        vmem((holders, tile, (MOST + 1) * LANES), BF16),
        vmem((tensors, rows, 2 * head), BF16),
        vmem((tensors, rows, 2 * head), BF16),
        dma((4 + 2 * per_holder,)),
        dma((5,)),
        dma((3 + 3 * CHUNKS,)),
    ]
    return pl.pallas_call(
        functools.partial(kernel, holders, tensors),
        out_shape=(
            jax.ShapeDtypeStruct((rows, features), BF16),
            jax.ShapeDtypeStruct((rows, head), BF16),
            jax.ShapeDtypeStruct((rows, head), BF16),
        ),
        in_specs=[pl.BlockSpec(memory_space=pl.ANY)] * 6,
        out_specs=tuple([pl.BlockSpec(memory_space=vmem)] * 3),
        scratch_shapes=scratch,
        compiler_params=pltpu.CompilerParams(
            collective_id=0, has_side_effects=True, vmem_limit_bytes=56 << 20
        ),
        name="adapters",
    )(tokens, index.reshape(1, rows), kv_weight, down, up_query, up_value)


def hand_over(*refs):
    count = len(refs) // 2
    for i in range(count):
        refs[count + i][...] = refs[i][...]


def local(holders, tensors, *operands):
    outs = step(holders, tensors, *operands)
    whole = [pl.BlockSpec(memory_space=pltpu.VMEM)] * len(outs)
    return pl.pallas_call(
        hand_over,
        out_shape=tuple(jax.ShapeDtypeStruct(o.shape, o.dtype) for o in outs),
        in_specs=whole,
        out_specs=tuple(whole),
        name="hand_over",
    )(*outs)


def solution(mesh):
    placed = (
        P("adapter", "tensor"),
        P("adapter", None),
        P("tensor", None, None),
        P("adapter", "tensor", None),
        P("adapter", None, "tensor"),
        P("adapter", None, "tensor"),
    )
    return jax.shard_map(
        functools.partial(local, mesh.shape["adapter"], mesh.shape["tensor"]),
        mesh=mesh,
        in_specs=placed,
        out_specs=(P("adapter", "tensor"), P("adapter", "tensor"), P("adapter", "tensor")),
        check_vma=False,
    )
```

```python
import functools
import jax
import jax.numpy as jnp
from jax import lax
from jax.experimental import pallas as pl
from jax.experimental.pallas import tpu as pltpu
from jax.sharding import PartitionSpec as P

MESH = pl.DeviceIdType.MESH
LANES = 128
BF16 = jnp.bfloat16
F32 = jnp.float32
MOST = 3
ZS, XS, CORES = 8, 4, 2
CHUNKS = XS
STEPS = (
    "a0", "b0", "a1", "c0", "b1", "a2", "a3", "b2", "c1", "b3", "c2", "s1", "v0", "v1", "v2",
    "c3", "v3", "f0", "f1", "f2", "base", "values", "f3",
)
BASE_TO = ((1, 7), (2, 6, 3, 5, 4))
R_BASE, R_V, R_TOK = 0, 1, 2
R_SUM, R_SHRUNK, R_RET, R_PAIR = (R_TOK + i * CHUNKS for i in range(1, 5))
S_TOK, S_BASE, S_SUM, S_SHRUNK, S_RET, S_PAIR, S_V = range(7)


def kernel(
    holders,
    tensors,
    tok_hbm,
    idx_hbm,
    kvw_hbm,
    down_hbm,
    upq_hbm,
    upv_hbm,
    q_out,
    k_out,
    v_out,
    tok,
    idx,
    kvw,
    wbase,
    lhs,
    down,
    up,
    fsel,
    fturn,
    vsel,
    stage,
    send,
    recv,
    xs,
    part,
    rs,
    sh,
    ustage,
    ret_send,
    ret_recv,
    ys,
    q_sum,
    v_all,
    v_pair,
    v_send,
    v_recv,
    bs_send,
    bs_recv,
    load_sems,
    send_sems,
    recv_sems,
):
    me = lax.axis_index("adapter")
    t = lax.axis_index("tensor")
    rows, features = tok.shape
    blocks = features // LANES
    per_holder = down.shape[0]
    adapters = holders * per_holder
    tile = per_holder * blocks
    chunk = holders // CHUNKS
    chunk_adapters = chunk * per_holder
    owners = MOST * per_holder
    z = me // (XS * CORES)
    x = (me // CORES) % XS
    core = me % CORES
    sibling = me + 1 - 2 * core
    self_pos = z * CORES + core

    def peer_of(p):
        offset = p // chunk
        px = (x + offset % 2 * (1 - 2 * (x % 2)) + 2 * (offset // 2)) % XS
        return ((p // CORES) % ZS) * (XS * CORES) + px * CORES + p % CORES

    def my_pos(p):
        return (p // chunk) * chunk + self_pos

    def for_peers(k, act):
        @pl.loop(1 if k == 0 else 0, chunk)
        def _(d):
            act(k * chunk + (self_pos + d) % chunk)

    def wait_bytes(ref, sem):
        pltpu.make_async_copy(ref, ref, sem).wait()

    def remote(src, dst, send_sem, recv_sem, device):
        return pltpu.make_async_remote_copy(
            src_ref=src,
            dst_ref=dst,
            send_sem=send_sems.at[send_sem],
            recv_sem=recv_sems.at[recv_sem],
            device_id=device,
            device_id_type=MESH,
        )

    get_tok = pltpu.make_async_copy(tok_hbm, tok, load_sems.at[0])
    get_idx = pltpu.make_async_copy(idx_hbm, idx, load_sems.at[1])
    get_kvw = pltpu.make_async_copy(kvw_hbm, kvw, load_sems.at[2])
    get_down = pltpu.make_async_copy(down_hbm, down, load_sems.at[3])
    get_idx.start()
    get_tok.start()

    barrier = pltpu.get_barrier_semaphore()

    @pl.loop(1, tensors, unroll=7)
    def _(d):
        pl.semaphore_signal(barrier, inc=1, device_id=(me, (t + d) % tensors), device_id_type=MESH)

    @pl.loop(1, holders, unroll=holders - 1)
    def _(d):
        pl.semaphore_signal(barrier, inc=1, device_id=((me + d) % holders, t), device_id_type=MESH)

    get_down.start()
    get_kvw.start()

    get_idx.wait()
    ids = idx[...]
    px = (ids >> 2) & 3
    offset = ((x + px) & 1) + 2 * (((x // 2) + (px >> 1)) & 1)
    place = offset * chunk_adapters + (ids >> 4) * (CORES * per_holder) + (ids & 3)
    places = lax.broadcasted_iota(jnp.int32, (adapters, rows), 0)
    picked = (places == place).astype(F32)
    earlier = lax.broadcasted_iota(jnp.int32, (rows, rows), 0) < lax.broadcasted_iota(
        jnp.int32, (rows, rows), 1
    )
    ordinal = jnp.dot(
        picked.astype(BF16), earlier.astype(F32).astype(BF16), preferred_element_type=F32
    )
    get_tok.wait()
    for m in range(MOST):
        chosen = jnp.where(ordinal == float(m), picked, 0.0)
        fsel[:, m * chunk_adapters : (m + 1) * chunk_adapters, :] = chosen.reshape(
            CHUNKS, chunk_adapters, rows
        )
        gathered = jnp.dot(chosen.astype(BF16), tok[...], preferred_element_type=F32)
        for j in range(blocks):
            stage[m, pl.ds(j, adapters, stride=blocks), :] = gathered[:, j * LANES : (j + 1) * LANES]
        send[:, :, m * LANES : (m + 1) * LANES] = (
            stage[m].reshape(holders, tile, LANES).astype(BF16)
        )

    pl.semaphore_wait(barrier, tensors - 1 + holders - 1)

    def dispatch_chunk(k):
        for_peers(
            k,
            lambda p: remote(
                send.at[p], recv.at[my_pos(p)], S_TOK, R_TOK + k, (peer_of(p), t)
            ).start(),
        )

    dispatch_chunk(0)
    recv[self_pos] = send[self_pos]

    up[...] = jnp.zeros_like(up)
    get_ups = []
    for a in range(per_holder):
        rank = upq_hbm.shape[1]
        get_ups.append(
            pltpu.make_async_copy(
                upq_hbm.at[a], up.at[a, pl.ds(0, rank), pl.ds(0, features)], load_sems.at[4 + a]
            )
        )
        get_ups.append(
            pltpu.make_async_copy(
                upv_hbm.at[a],
                up.at[a, pl.ds(rank, rank), pl.ds(features, LANES)],
                load_sems.at[4 + per_holder + a],
            )
        )
    for copy in get_ups:
        copy.start()
    for c in range(2):
        spread = (
            lax.broadcasted_iota(jnp.int32, (LANES, 2 * LANES), 1)
            == 2 * lax.broadcasted_iota(jnp.int32, (LANES, 2 * LANES), 0) + c
        ).astype(F32).astype(BF16)
        for j in range(blocks):
            lhs[c, :, 2 * j * LANES : 2 * (j + 1) * LANES] = jnp.dot(
                tok[:, j * LANES : (j + 1) * LANES], spread, preferred_element_type=F32
            ).astype(BF16)
    dispatch_chunk(1)
    get_kvw.wait()
    run = 32

    @pl.loop(0, features // run)
    def _(i):
        wbase[pl.ds(i * 2 * run, 2 * run), :] = kvw[pl.ds(i * run, run)].reshape(
            2 * run, wbase.shape[1]
        )

    dispatch_chunk(2)
    @pl.loop(0, tensors // 2)
    def _(n):
        columns = pl.ds(pl.multiple_of(n * 2 * LANES, 2 * LANES), 2 * LANES)
        for c in range(2):
            terms = jnp.dot(lhs[c], wbase[:, columns], preferred_element_type=F32).astype(BF16)
            for half in range(2):
                bs_send[2 * n + half, :, c * LANES : (c + 1) * LANES] = terms[
                    :, half * LANES : (half + 1) * LANES
                ]

    dispatch_chunk(3)

    def base_sends(ds):
        for d in ds:
            other = (t + d) % tensors
            remote(bs_send.at[other], bs_recv.at[t], S_BASE, R_BASE, (me, other)).start()

    base_sends(BASE_TO[0])
    bs_recv[t] = bs_send[t]
    ustage[MOST] = jnp.zeros_like(ustage[MOST])
    for k in range(CHUNKS):
        fturn[k] = fsel[k].T.astype(BF16)
    pairs = adapters // (CORES * per_holder)
    turned = (places == (place & 3) * pairs + (place >> 2)).astype(F32)
    turned_ordinal = jnp.dot(
        turned.astype(BF16), earlier.astype(F32).astype(BF16), preferred_element_type=F32
    )
    for m in range(MOST):
        chosen = jnp.where(turned_ordinal == float(m), turned, 0.0)
        vsel[:, m * adapters : (m + 1) * adapters] = chosen.T.astype(BF16)
    get_down.wait()
    for copy in get_ups:
        copy.wait()

    def arrive(k):
        wait_bytes(recv.at[pl.ds(0, chunk - 1 if k == 0 else chunk)], recv_sems.at[R_TOK + k])
        for m in range(MOST):
            stage[m, pl.ds(0, chunk * tile), :] = (
                recv[pl.ds(k * chunk, chunk), :, m * LANES : (m + 1) * LANES]
                .astype(F32)
                .reshape(chunk * tile, LANES)
            )
        for a in range(per_holder):
            for m in range(MOST):
                for j in range(blocks):
                    xs[a, m * chunk : (m + 1) * chunk, j * LANES : (j + 1) * LANES] = stage[
                        m, pl.ds(a * blocks + j, chunk, stride=tile), :
                    ].astype(BF16)
            terms = jnp.dot(xs[a], down[a], preferred_element_type=F32)
            for m in range(MOST):
                part[k, a * MOST + m] = terms[m * chunk : (m + 1) * chunk]

        @pl.loop(1, tensors)
        def _(d):
            other = (t + d) % tensors

            @pl.when(other < owners)
            def _():
                remote(part.at[k, other], rs.at[k, t], S_SUM, R_SUM + k, (me, other)).start()

    def total(k):
        @pl.when(t < owners)
        def _():
            rs[k, t] = part[k, t]
            wait_bytes(rs.at[k, pl.ds(0, tensors - 1)], recv_sems.at[R_SUM + k])
            summed = rs[k, 0]
            for s in range(1, tensors):
                summed = summed + rs[k, s]
            sh[k, t] = summed.astype(BF16)

            @pl.loop(1, tensors)
            def _(d):
                other = (t + d) % tensors
                remote(sh.at[k, t], sh.at[k, t], S_SHRUNK, R_SHRUNK + k, (me, other)).start()

    def corrections(k):
        @pl.when(t < owners)
        def _():
            wait_bytes(sh.at[k, pl.ds(0, owners - 1)], recv_sems.at[R_SHRUNK + k])

        @pl.when(t >= owners)
        def _():
            wait_bytes(sh.at[k, pl.ds(0, owners)], recv_sems.at[R_SHRUNK + k])

        for a in range(per_holder):
            shrunk = sh[k, a * MOST : (a + 1) * MOST].reshape(MOST * chunk, LANES)
            deltas = jnp.dot(shrunk, up[a], preferred_element_type=F32)
            for m in range(MOST):
                of_m = deltas[m * chunk : (m + 1) * chunk]
                for j in range(blocks):
                    ustage[m, pl.ds(a * blocks + j, chunk, stride=tile), :] = of_m[
                        :, j * LANES : (j + 1) * LANES
                    ]
                ustage[
                    MOST, pl.ds(a * blocks + m + core * (blocks // 2), chunk, stride=tile), :
                ] = of_m[:, features:]
        v_all[k] = ustage[MOST].reshape(ZS, CORES, tile, LANES).astype(BF16)
        remote(
            v_all.at[k, :, 1 - core], v_pair.at[k], S_PAIR, R_PAIR + k, (sibling, t)
        ).start()
        for m in range(MOST):
            ret_send[pl.ds(k * chunk, chunk), :, m * LANES : (m + 1) * LANES] = (
                ustage[m].reshape(chunk, tile, LANES).astype(BF16)
            )
        for_peers(
            k,
            lambda p: remote(
                ret_send.at[p], ret_recv.at[my_pos(p)], S_RET, R_RET + k, (peer_of(p), t)
            ).start(),
        )
        if k == 0:
            ret_recv[self_pos] = ret_send[self_pos]

    def value_tiles(k):
        wait_bytes(v_pair.at[k], recv_sems.at[R_PAIR + k])
        v_send[k] = v_all[k, :, core] + v_pair[k]

        @pl.loop(1 if k == 0 else 0, ZS)
        def _(d):
            to = (z + d) % ZS
            p = k * chunk + to * CORES + core
            remote(v_send.at[k, to], v_recv.at[k * ZS + z], S_V, R_V, (peer_of(p), t)).start()

        if k == 0:
            v_recv[z] = v_send[k, z]

    def base_sum():
        wait_bytes(bs_recv.at[pl.ds(0, tensors - 1)], recv_sems.at[R_BASE])
        base = bs_recv[0].astype(F32)
        for s in range(1, tensors):
            base = base + bs_recv[s].astype(F32)
        k_out[...] = base[:, :LANES].astype(BF16)
        return base[:, LANES:]

    def select_back(k):
        wait_bytes(
            ret_recv.at[pl.ds(0, chunk - 1 if k == 0 else chunk)], recv_sems.at[R_RET + k]
        )
        for m in range(MOST):
            stage[m, pl.ds(0, chunk * tile), :] = (
                ret_recv[pl.ds(k * chunk, chunk), :, m * LANES : (m + 1) * LANES]
                .astype(F32)
                .reshape(chunk * tile, LANES)
            )
            for j in range(blocks):
                ys[
                    m * chunk_adapters : (m + 1) * chunk_adapters, j * LANES : (j + 1) * LANES
                ] = stage[m, pl.ds(j, chunk_adapters, stride=blocks), :].astype(BF16)
        found = jnp.dot(fturn[k], ys[...], preferred_element_type=F32)
        if k == 0:
            q_sum[...] = found
        elif k < CHUNKS - 1:
            q_sum[...] += found
        else:
            q_out[...] = (q_sum[...] + found).astype(BF16)

    def add_values(base_values):
        wait_bytes(v_recv.at[pl.ds(0, pairs - 1)], recv_sems.at[R_V])
        stage[0, pl.ds(0, pairs * tile), :] = v_recv[...].astype(F32).reshape(pairs * tile, LANES)
        gathered = jnp.concatenate(
            [
                stage[0, pl.ds(a * blocks + c * (blocks // 2) + m, pairs, stride=tile), :]
                for m in range(MOST)
                for c in range(CORES)
                for a in range(per_holder)
            ],
            axis=0,
        ).astype(BF16)
        v_out[...] = (
            base_values + jnp.dot(vsel[...], gathered, preferred_element_type=F32)
        ).astype(BF16)

    base_values = None
    for name in STEPS:
        if name == "base":
            base_values = base_sum()
        elif name == "values":
            add_values(base_values)
        else:
            of = {
                "a": arrive,
                "b": total,
                "c": corrections,
                "v": value_tiles,
                "f": select_back,
                "s": lambda k: base_sends(BASE_TO[k]),
            }
            of[name[0]](int(name[1]))

    wait_bytes(send.at[pl.ds(0, holders - 1)], send_sems.at[S_TOK])
    wait_bytes(bs_send.at[pl.ds(0, tensors - 1)], send_sems.at[S_BASE])

    @pl.when(t < owners)
    def _():
        for k in range(CHUNKS):
            wait_bytes(part.at[k, pl.ds(0, owners - 1)], send_sems.at[S_SUM])
            wait_bytes(
                rs.at[k, pl.ds(0, tensors - 1), pl.ds(0, chunk // 2)], send_sems.at[S_SHRUNK]
            )

    @pl.when(t >= owners)
    def _():
        for k in range(CHUNKS):
            wait_bytes(part.at[k, pl.ds(0, owners)], send_sems.at[S_SUM])

    wait_bytes(ret_send.at[pl.ds(0, holders - 1)], send_sems.at[S_RET])
    wait_bytes(v_pair, send_sems.at[S_PAIR])
    wait_bytes(v_recv.at[pl.ds(0, pairs - 1)], send_sems.at[S_V])


def step(holders, tensors, tokens, index, kv_weight, down, up_query, up_value):
    rows, features = tokens.shape
    head = kv_weight.shape[2] // tensors
    per_holder = down.shape[0]
    blocks = features // LANES
    tile = per_holder * blocks
    chunk = holders // CHUNKS
    owners = MOST * per_holder
    adapters = holders * per_holder
    pairs = holders // CORES
    vmem = pltpu.VMEM
    dma = pltpu.SemaphoreType.DMA
    scratch = [
        vmem(tokens.shape, BF16),
        vmem((1, rows), jnp.int32),
        vmem(kv_weight.shape, BF16),
        vmem((2 * features, kv_weight.shape[2]), BF16),
        vmem((2, rows, 2 * features), BF16),
        vmem(down.shape, BF16),
        vmem((per_holder, 2 * up_query.shape[1], features + LANES), BF16),
        vmem((CHUNKS, MOST * chunk * per_holder, rows), F32),
        vmem((CHUNKS, rows, MOST * chunk * per_holder), BF16),
        vmem((rows, MOST * adapters), BF16),
        vmem((MOST, holders * tile, LANES), F32),
        vmem((holders, tile, MOST * LANES), BF16),
        vmem((holders, tile, MOST * LANES), BF16),
        vmem((per_holder, MOST * chunk, features), BF16),
        vmem((CHUNKS, owners, chunk, LANES), F32),
        vmem((CHUNKS, tensors, chunk, LANES), F32),
        vmem((CHUNKS, owners, chunk, LANES), BF16),
        vmem((MOST + 1, chunk * tile, LANES), F32),
        vmem((holders, tile, MOST * LANES), BF16),
        vmem((holders, tile, MOST * LANES), BF16),
        vmem((MOST * chunk * per_holder, features), BF16),
        vmem((rows, features), F32),
        vmem((CHUNKS, ZS, CORES, tile, LANES), BF16),
        vmem((CHUNKS, ZS, tile, LANES), BF16),
        vmem((CHUNKS, ZS, tile, LANES), BF16),
        vmem((pairs, tile, LANES), BF16),
        vmem((tensors, rows, 2 * head), BF16),
        vmem((tensors, rows, 2 * head), BF16),
        dma((4 + 2 * per_holder,)),
        dma((7,)),
        dma((R_TOK + 5 * CHUNKS,)),
    ]
    return pl.pallas_call(
        functools.partial(kernel, holders, tensors),
        out_shape=(
            vmem((rows, features), BF16),
            vmem((rows, head), BF16),
            vmem((rows, head), BF16),
        ),
        in_specs=[pl.BlockSpec(memory_space=pltpu.HBM)] * 6,
        out_specs=tuple([pl.BlockSpec(memory_space=vmem)] * 3),
        scratch_shapes=scratch,
        compiler_params=pltpu.CompilerParams(
            collective_id=0, has_side_effects=True, vmem_limit_bytes=24 << 20
        ),
        name="adapters",
    )(
        *[
            pltpu.with_memory_space_constraint(operand, pltpu.HBM)
            for operand in (tokens, index.reshape(1, rows), kv_weight, down, up_query, up_value)
        ]
    )


def hand_over(*refs):
    count = len(refs) // 2
    copies = [
        pltpu.make_async_copy(refs[i], refs[count + i], refs[-1].at[i]) for i in range(count)
    ]
    for copy in copies:
        copy.start()
    for copy in copies:
        copy.wait()


def local(holders, tensors, *operands):
    outs = step(holders, tensors, *operands)
    return pl.pallas_call(
        hand_over,
        out_shape=tuple(jax.ShapeDtypeStruct(o.shape, o.dtype) for o in outs),
        in_specs=[pl.BlockSpec(memory_space=pltpu.VMEM)] * len(outs),
        out_specs=tuple([pl.BlockSpec(memory_space=pltpu.HBM)] * len(outs)),
        scratch_shapes=[pltpu.SemaphoreType.DMA((len(outs),))],
        compiler_params=pltpu.CompilerParams(vmem_limit_bytes=2 << 20),
        name="hand_over",
    )(*outs)


def solution(mesh):
    placed = (
        P("adapter", "tensor"),
        P("adapter", None),
        P("tensor", None, None),
        P("adapter", "tensor", None),
        P("adapter", None, "tensor"),
        P("adapter", None, "tensor"),
    )
    return jax.shard_map(
        functools.partial(local, mesh.shape["adapter"], mesh.shape["tensor"]),
        mesh=mesh,
        in_specs=placed,
        out_specs=(P("adapter", "tensor"), P("adapter", "tensor"), P("adapter", "tensor")),
        check_vma=False,
    )
```

```python
import functools
import jax
import jax.numpy as jnp
from jax import lax
from jax.experimental import pallas as pl
from jax.experimental.pallas import tpu as pltpu
from jax.sharding import PartitionSpec as P

MESH = pl.DeviceIdType.MESH
LANES = 128
BF16 = jnp.bfloat16
F32 = jnp.float32
MOST = 3
ZS, XS, CORES = 8, 4, 2
CHUNKS = XS
Z_AWAY = (4, 3, 5, 2, 6, 1, 7, 0)
Y_AWAY = (4, 3, 5, 2, 6, 1, 7)
STEPS = (
    "a0", "b0", "a1", "c0", "b1", "a2", "a3", "b2", "c1", "b3", "c2", "s1", "v0", "v1", "v2",
    "c3", "v3", "f0", "f1", "f2", "base", "values", "f3",
)
BASE_TO = ((1, 7), (2, 6, 3, 5, 4))
R_BASE, R_V, R_TOK = 0, 1, 2
R_SUM, R_SHRUNK, R_RET, R_PAIR = (R_TOK + i * CHUNKS for i in range(1, 5))
S_TOK, S_BASE, S_SUM, S_SHRUNK, S_RET, S_PAIR, S_V = range(7)


def kernel(
    holders,
    tensors,
    tok_hbm,
    idx_hbm,
    kvw_hbm,
    down_hbm,
    upq_hbm,
    upv_hbm,
    q_out,
    k_out,
    v_out,
    tok,
    idx,
    kvw,
    wbase,
    lhs,
    down,
    up,
    fsel,
    fturn,
    vsel,
    stage,
    send,
    recv,
    xs,
    part,
    rs,
    sh,
    ustage,
    ret_send,
    ret_recv,
    ys,
    q_sum,
    v_all,
    v_pair,
    v_send,
    v_recv,
    bs_send,
    bs_recv,
    load_sems,
    send_sems,
    recv_sems,
):
    me = lax.axis_index("adapter")
    t = lax.axis_index("tensor")
    rows, features = tok.shape
    blocks = features // LANES
    per_holder = down.shape[0]
    adapters = holders * per_holder
    tile = per_holder * blocks
    chunk = holders // CHUNKS
    chunk_adapters = chunk * per_holder
    owners = MOST * per_holder
    z = me // (XS * CORES)
    x = (me // CORES) % XS
    core = me % CORES
    sibling = me + 1 - 2 * core
    self_pos = z * CORES + core

    def for_peers(k, cores, act):
        px = (x + k % 2 * (1 - 2 * (x % 2)) + 2 * (k // 2)) % XS
        for dz in Z_AWAY:
            pz = (z + dz) % ZS
            for dc in cores:
                if (k, dz, dc) != (0, 0, 0):
                    pc = (core + dc) % CORES
                    act(
                        k * chunk + pz * CORES + pc,
                        k * chunk + self_pos,
                        (pz * XS + px) * CORES + pc,
                    )

    def wait_bytes(ref, sem):
        pltpu.make_async_copy(ref, ref, sem).wait()

    def remote(src, dst, send_sem, recv_sem, device):
        return pltpu.make_async_remote_copy(
            src_ref=src,
            dst_ref=dst,
            send_sem=send_sems.at[send_sem],
            recv_sem=recv_sems.at[recv_sem],
            device_id=device,
            device_id_type=MESH,
        )

    get_tok = pltpu.make_async_copy(tok_hbm, tok, load_sems.at[0])
    get_idx = pltpu.make_async_copy(idx_hbm, idx, load_sems.at[1])
    get_kvw = pltpu.make_async_copy(kvw_hbm, kvw, load_sems.at[2])
    get_down = pltpu.make_async_copy(down_hbm, down, load_sems.at[3])
    get_idx.start()
    get_tok.start()

    barrier = pltpu.get_barrier_semaphore()

    for dz in Z_AWAY:
        for d in range(XS * CORES):
            if (dz, d) != (0, 0):
                to = (z + dz) % ZS * (XS * CORES) + (me + d) % (XS * CORES)
                pl.semaphore_signal(barrier, inc=1, device_id=(to, t), device_id_type=MESH)
    for d in Y_AWAY:
        pl.semaphore_signal(barrier, inc=1, device_id=(me, (t + d) % tensors), device_id_type=MESH)

    get_down.start()
    get_kvw.start()

    get_idx.wait()
    ids = idx[...]
    px = (ids >> 2) & 3
    offset = ((x + px) & 1) + 2 * (((x // 2) + (px >> 1)) & 1)
    place = offset * chunk_adapters + (ids >> 4) * (CORES * per_holder) + (ids & 3)
    places = lax.broadcasted_iota(jnp.int32, (adapters, rows), 0)
    picked = (places == place).astype(F32)
    earlier = lax.broadcasted_iota(jnp.int32, (rows, rows), 0) < lax.broadcasted_iota(
        jnp.int32, (rows, rows), 1
    )
    ordinal = jnp.dot(
        picked.astype(BF16), earlier.astype(F32).astype(BF16), preferred_element_type=F32
    )
    get_tok.wait()
    for m in range(MOST):
        chosen = jnp.where(ordinal == float(m), picked, 0.0)
        fsel[:, m * chunk_adapters : (m + 1) * chunk_adapters, :] = chosen.reshape(
            CHUNKS, chunk_adapters, rows
        )
        gathered = jnp.dot(chosen.astype(BF16), tok[...], preferred_element_type=F32)
        for j in range(blocks):
            stage[m, pl.ds(j, adapters, stride=blocks), :] = gathered[:, j * LANES : (j + 1) * LANES]
        send[:, :, m * LANES : (m + 1) * LANES] = (
            stage[m].reshape(holders, tile, LANES).astype(BF16)
        )

    pl.semaphore_wait(barrier, tensors - 1 + holders - 1)

    def dispatch_chunk(k):
        for_peers(
            k,
            (1, 0),
            lambda at, there, to: remote(
                send.at[at], recv.at[there], S_TOK, R_TOK + k, (to, t)
            ).start(),
        )

    dispatch_chunk(0)
    recv[self_pos] = send[self_pos]

    up[...] = jnp.zeros_like(up)
    get_ups = []
    for a in range(per_holder):
        rank = upq_hbm.shape[1]
        get_ups.append(
            pltpu.make_async_copy(
                upq_hbm.at[a], up.at[a, pl.ds(0, rank), pl.ds(0, features)], load_sems.at[4 + a]
            )
        )
        get_ups.append(
            pltpu.make_async_copy(
                upv_hbm.at[a],
                up.at[a, pl.ds(rank, rank), pl.ds(features, LANES)],
                load_sems.at[4 + per_holder + a],
            )
        )
    for copy in get_ups:
        copy.start()
    for c in range(2):
        spread = (
            lax.broadcasted_iota(jnp.int32, (LANES, 2 * LANES), 1)
            == 2 * lax.broadcasted_iota(jnp.int32, (LANES, 2 * LANES), 0) + c
        ).astype(F32).astype(BF16)
        for j in range(blocks):
            lhs[c, :, 2 * j * LANES : 2 * (j + 1) * LANES] = jnp.dot(
                tok[:, j * LANES : (j + 1) * LANES], spread, preferred_element_type=F32
            ).astype(BF16)
    dispatch_chunk(1)
    get_kvw.wait()
    run = 32

    @pl.loop(0, features // run)
    def _(i):
        wbase[pl.ds(i * 2 * run, 2 * run), :] = kvw[pl.ds(i * run, run)].reshape(
            2 * run, wbase.shape[1]
        )

    dispatch_chunk(2)
    @pl.loop(0, tensors // 2)
    def _(n):
        columns = pl.ds(pl.multiple_of(n * 2 * LANES, 2 * LANES), 2 * LANES)
        for c in range(2):
            terms = jnp.dot(lhs[c], wbase[:, columns], preferred_element_type=F32).astype(BF16)
            for half in range(2):
                bs_send[2 * n + half, :, c * LANES : (c + 1) * LANES] = terms[
                    :, half * LANES : (half + 1) * LANES
                ]

    dispatch_chunk(3)

    def base_sends(ds):
        for d in ds:
            other = (t + d) % tensors
            remote(bs_send.at[other], bs_recv.at[t], S_BASE, R_BASE, (me, other)).start()

    base_sends(BASE_TO[0])
    bs_recv[t] = bs_send[t]
    ustage[MOST] = jnp.zeros_like(ustage[MOST])
    for k in range(CHUNKS):
        fturn[k] = fsel[k].T.astype(BF16)
    pairs = adapters // (CORES * per_holder)
    turned = (places == (place & 3) * pairs + (place >> 2)).astype(F32)
    turned_ordinal = jnp.dot(
        turned.astype(BF16), earlier.astype(F32).astype(BF16), preferred_element_type=F32
    )
    for m in range(MOST):
        chosen = jnp.where(turned_ordinal == float(m), turned, 0.0)
        vsel[:, m * adapters : (m + 1) * adapters] = chosen.T.astype(BF16)
    get_down.wait()
    for copy in get_ups:
        copy.wait()

    def arrive(k):
        wait_bytes(recv.at[pl.ds(0, chunk - 1 if k == 0 else chunk)], recv_sems.at[R_TOK + k])
        for m in range(MOST):
            stage[m, pl.ds(0, chunk * tile), :] = (
                recv[pl.ds(k * chunk, chunk), :, m * LANES : (m + 1) * LANES]
                .astype(F32)
                .reshape(chunk * tile, LANES)
            )
        for a in range(per_holder):
            for m in range(MOST):
                for j in range(blocks):
                    xs[a, m * chunk : (m + 1) * chunk, j * LANES : (j + 1) * LANES] = stage[
                        m, pl.ds(a * blocks + j, chunk, stride=tile), :
                    ].astype(BF16)
            terms = jnp.dot(xs[a], down[a], preferred_element_type=F32)
            for m in range(MOST):
                part[k, a * MOST + m] = terms[m * chunk : (m + 1) * chunk]

        for d in Y_AWAY:
            other = (t + d) % tensors

            @pl.when(other < owners)
            def _():
                remote(part.at[k, other], rs.at[k, t], S_SUM, R_SUM + k, (me, other)).start()

    def total(k):
        @pl.when(t < owners)
        def _():
            rs[k, t] = part[k, t]
            wait_bytes(rs.at[k, pl.ds(0, tensors - 1)], recv_sems.at[R_SUM + k])
            summed = rs[k, 0]
            for s in range(1, tensors):
                summed = summed + rs[k, s]
            sh[k, t] = summed.astype(BF16)

            for d in Y_AWAY:
                other = (t + d) % tensors
                remote(sh.at[k, t], sh.at[k, t], S_SHRUNK, R_SHRUNK + k, (me, other)).start()

    def corrections(k):
        @pl.when(t < owners)
        def _():
            wait_bytes(sh.at[k, pl.ds(0, owners - 1)], recv_sems.at[R_SHRUNK + k])

        @pl.when(t >= owners)
        def _():
            wait_bytes(sh.at[k, pl.ds(0, owners)], recv_sems.at[R_SHRUNK + k])

        for a in range(per_holder):
            shrunk = sh[k, a * MOST : (a + 1) * MOST].reshape(MOST * chunk, LANES)
            deltas = jnp.dot(shrunk, up[a], preferred_element_type=F32)
            for m in range(MOST):
                of_m = deltas[m * chunk : (m + 1) * chunk]
                for j in range(blocks):
                    ustage[m, pl.ds(a * blocks + j, chunk, stride=tile), :] = of_m[
                        :, j * LANES : (j + 1) * LANES
                    ]
                ustage[
                    MOST, pl.ds(a * blocks + m + core * (blocks // 2), chunk, stride=tile), :
                ] = of_m[:, features:]
        v_all[k] = ustage[MOST].reshape(ZS, CORES, tile, LANES).astype(BF16)
        remote(
            v_all.at[k, :, 1 - core], v_pair.at[k], S_PAIR, R_PAIR + k, (sibling, t)
        ).start()
        for m in range(MOST):
            ret_send[pl.ds(k * chunk, chunk), :, m * LANES : (m + 1) * LANES] = (
                ustage[m].reshape(chunk, tile, LANES).astype(BF16)
            )
        for_peers(
            k,
            (1, 0),
            lambda at, there, to: remote(
                ret_send.at[at], ret_recv.at[there], S_RET, R_RET + k, (to, t)
            ).start(),
        )
        if k == 0:
            ret_recv[self_pos] = ret_send[self_pos]

    def value_tiles(k):
        wait_bytes(v_pair.at[k], recv_sems.at[R_PAIR + k])
        v_send[k] = v_all[k, :, core] + v_pair[k]

        for_peers(
            k,
            (0,),
            lambda at, there, to: remote(
                v_send.at[k, at // CORES - k * ZS], v_recv.at[there // CORES], S_V, R_V, (to, t)
            ).start(),
        )
        if k == 0:
            v_recv[z] = v_send[k, z]

    def base_sum():
        wait_bytes(bs_recv.at[pl.ds(0, tensors - 1)], recv_sems.at[R_BASE])
        base = bs_recv[0].astype(F32)
        for s in range(1, tensors):
            base = base + bs_recv[s].astype(F32)
        k_out[...] = base[:, :LANES].astype(BF16)
        return base[:, LANES:]

    def select_back(k):
        wait_bytes(
            ret_recv.at[pl.ds(0, chunk - 1 if k == 0 else chunk)], recv_sems.at[R_RET + k]
        )
        for m in range(MOST):
            stage[m, pl.ds(0, chunk * tile), :] = (
                ret_recv[pl.ds(k * chunk, chunk), :, m * LANES : (m + 1) * LANES]
                .astype(F32)
                .reshape(chunk * tile, LANES)
            )
            for j in range(blocks):
                ys[
                    m * chunk_adapters : (m + 1) * chunk_adapters, j * LANES : (j + 1) * LANES
                ] = stage[m, pl.ds(j, chunk_adapters, stride=blocks), :].astype(BF16)
        found = jnp.dot(fturn[k], ys[...], preferred_element_type=F32)
        if k == 0:
            q_sum[...] = found
        elif k < CHUNKS - 1:
            q_sum[...] += found
        else:
            q_out[...] = (q_sum[...] + found).astype(BF16)

    def add_values(base_values):
        wait_bytes(v_recv.at[pl.ds(0, pairs - 1)], recv_sems.at[R_V])
        stage[0, pl.ds(0, pairs * tile), :] = v_recv[...].astype(F32).reshape(pairs * tile, LANES)
        gathered = jnp.concatenate(
            [
                stage[0, pl.ds(a * blocks + c * (blocks // 2) + m, pairs, stride=tile), :]
                for m in range(MOST)
                for c in range(CORES)
                for a in range(per_holder)
            ],
            axis=0,
        ).astype(BF16)
        v_out[...] = (
            base_values + jnp.dot(vsel[...], gathered, preferred_element_type=F32)
        ).astype(BF16)

    base_values = None
    for name in STEPS:
        if name == "base":
            base_values = base_sum()
        elif name == "values":
            add_values(base_values)
        else:
            of = {
                "a": arrive,
                "b": total,
                "c": corrections,
                "v": value_tiles,
                "f": select_back,
                "s": lambda k: base_sends(BASE_TO[k]),
            }
            of[name[0]](int(name[1]))

    wait_bytes(send.at[pl.ds(0, holders - 1)], send_sems.at[S_TOK])
    wait_bytes(bs_send.at[pl.ds(0, tensors - 1)], send_sems.at[S_BASE])

    @pl.when(t < owners)
    def _():
        for k in range(CHUNKS):
            wait_bytes(part.at[k, pl.ds(0, owners - 1)], send_sems.at[S_SUM])
            wait_bytes(
                rs.at[k, pl.ds(0, tensors - 1), pl.ds(0, chunk // 2)], send_sems.at[S_SHRUNK]
            )

    @pl.when(t >= owners)
    def _():
        for k in range(CHUNKS):
            wait_bytes(part.at[k, pl.ds(0, owners)], send_sems.at[S_SUM])

    wait_bytes(ret_send.at[pl.ds(0, holders - 1)], send_sems.at[S_RET])
    wait_bytes(v_pair, send_sems.at[S_PAIR])
    wait_bytes(v_recv.at[pl.ds(0, pairs - 1)], send_sems.at[S_V])


def step(holders, tensors, tokens, index, kv_weight, down, up_query, up_value):
    rows, features = tokens.shape
    head = kv_weight.shape[2] // tensors
    per_holder = down.shape[0]
    blocks = features // LANES
    tile = per_holder * blocks
    chunk = holders // CHUNKS
    owners = MOST * per_holder
    adapters = holders * per_holder
    pairs = holders // CORES
    vmem = pltpu.VMEM
    dma = pltpu.SemaphoreType.DMA
    scratch = [
        vmem(tokens.shape, BF16),
        vmem((1, rows), jnp.int32),
        vmem(kv_weight.shape, BF16),
        vmem((2 * features, kv_weight.shape[2]), BF16),
        vmem((2, rows, 2 * features), BF16),
        vmem(down.shape, BF16),
        vmem((per_holder, 2 * up_query.shape[1], features + LANES), BF16),
        vmem((CHUNKS, MOST * chunk * per_holder, rows), F32),
        vmem((CHUNKS, rows, MOST * chunk * per_holder), BF16),
        vmem((rows, MOST * adapters), BF16),
        vmem((MOST, holders * tile, LANES), F32),
        vmem((holders, tile, MOST * LANES), BF16),
        vmem((holders, tile, MOST * LANES), BF16),
        vmem((per_holder, MOST * chunk, features), BF16),
        vmem((CHUNKS, owners, chunk, LANES), F32),
        vmem((CHUNKS, tensors, chunk, LANES), F32),
        vmem((CHUNKS, owners, chunk, LANES), BF16),
        vmem((MOST + 1, chunk * tile, LANES), F32),
        vmem((holders, tile, MOST * LANES), BF16),
        vmem((holders, tile, MOST * LANES), BF16),
        vmem((MOST * chunk * per_holder, features), BF16),
        vmem((rows, features), F32),
        vmem((CHUNKS, ZS, CORES, tile, LANES), BF16),
        vmem((CHUNKS, ZS, tile, LANES), BF16),
        vmem((CHUNKS, ZS, tile, LANES), BF16),
        vmem((pairs, tile, LANES), BF16),
        vmem((tensors, rows, 2 * head), BF16),
        vmem((tensors, rows, 2 * head), BF16),
        dma((4 + 2 * per_holder,)),
        dma((7,)),
        dma((R_TOK + 5 * CHUNKS,)),
    ]
    return pl.pallas_call(
        functools.partial(kernel, holders, tensors),
        out_shape=(
            vmem((rows, features), BF16),
            vmem((rows, head), BF16),
            vmem((rows, head), BF16),
        ),
        in_specs=[pl.BlockSpec(memory_space=pltpu.HBM)] * 6,
        out_specs=tuple([pl.BlockSpec(memory_space=vmem)] * 3),
        scratch_shapes=scratch,
        compiler_params=pltpu.CompilerParams(
            collective_id=0, has_side_effects=True, vmem_limit_bytes=24 << 20
        ),
        name="adapters",
    )(
        *[
            pltpu.with_memory_space_constraint(operand, pltpu.HBM)
            for operand in (tokens, index.reshape(1, rows), kv_weight, down, up_query, up_value)
        ]
    )


def hand_over(*refs):
    count = len(refs) // 2
    copies = [
        pltpu.make_async_copy(refs[i], refs[count + i], refs[-1].at[i]) for i in range(count)
    ]
    for copy in copies:
        copy.start()
    for copy in copies:
        copy.wait()


def local(holders, tensors, *operands):
    outs = step(holders, tensors, *operands)
    return pl.pallas_call(
        hand_over,
        out_shape=tuple(jax.ShapeDtypeStruct(o.shape, o.dtype) for o in outs),
        in_specs=[pl.BlockSpec(memory_space=pltpu.VMEM)] * len(outs),
        out_specs=tuple([pl.BlockSpec(memory_space=pltpu.HBM)] * len(outs)),
        scratch_shapes=[pltpu.SemaphoreType.DMA((len(outs),))],
        compiler_params=pltpu.CompilerParams(vmem_limit_bytes=2 << 20),
        name="hand_over",
    )(*outs)


def solution(mesh):
    placed = (
        P("adapter", "tensor"),
        P("adapter", None),
        P("tensor", None, None),
        P("adapter", "tensor", None),
        P("adapter", None, "tensor"),
        P("adapter", None, "tensor"),
    )
    return jax.shard_map(
        functools.partial(local, mesh.shape["adapter"], mesh.shape["tensor"]),
        mesh=mesh,
        in_specs=placed,
        out_specs=(P("adapter", "tensor"), P("adapter", "tensor"), P("adapter", "tensor")),
        check_vma=False,
    )
```

```python
import functools
import jax
import jax.numpy as jnp
from jax import lax
from jax.experimental import pallas as pl
from jax.experimental.pallas import tpu as pltpu
from jax.sharding import PartitionSpec as P

MESH = pl.DeviceIdType.MESH
LANES = 128
BF16 = jnp.bfloat16
F32 = jnp.float32
MOST = 3
ZS, XS, CORES = 8, 4, 2
CHUNKS = XS
Z_AWAY = (4, 3, 5, 2, 6, 1, 7, 0)
Y_AWAY = (4, 3, 5, 2, 6, 1, 7)
STEPS = (
    "a0", "b0", "a1", "c0", "b1", "a2", "a3", "b2", "c1", "b3", "c2", "s1", "v0", "v1", "v2",
    "c3", "v3", "f0", "f1", "f2", "base", "values", "f3",
)
BASE_TO = ((1, 7), (2, 6, 3, 5, 4))
R_BASE, R_V, R_TOK = 0, 1, 2
R_SUM, R_SHRUNK, R_RET, R_PAIR = (R_TOK + i * CHUNKS for i in range(1, 5))
S_TOK, S_BASE, S_SUM, S_SHRUNK, S_RET, S_PAIR, S_V = range(7)


def kernel(
    holders,
    tensors,
    tok_hbm,
    idx_hbm,
    kvw_hbm,
    down_hbm,
    upq_hbm,
    upv_hbm,
    q_out,
    k_out,
    v_out,
    tok,
    idx,
    kvw,
    wbase,
    lhs,
    down,
    up,
    fsel,
    fturn,
    vsel,
    stage,
    send,
    recv,
    xs,
    part,
    rs,
    sh,
    ustage,
    ret_send,
    ret_recv,
    ys,
    q_sum,
    v_all,
    v_pair,
    v_send,
    v_recv,
    bs_send,
    bs_recv,
    load_sems,
    send_sems,
    recv_sems,
):
    me = lax.axis_index("adapter")
    t = lax.axis_index("tensor")
    rows, features = tok.shape
    blocks = features // LANES
    per_holder = down.shape[0]
    adapters = holders * per_holder
    tile = per_holder * blocks
    chunk = holders // CHUNKS
    chunk_adapters = chunk * per_holder
    owners = MOST * per_holder
    z = me // (XS * CORES)
    x = (me // CORES) % XS
    core = me % CORES
    sibling = me + 1 - 2 * core
    self_pos = z * CORES + core

    def for_peers(k, cores, act):
        px = (x + k % 2 * (1 - 2 * (x % 2)) + 2 * (k // 2)) % XS
        for dz in Z_AWAY:
            pz = (z + dz) % ZS
            for dc in cores:
                if (k, dz, dc) != (0, 0, 0):
                    pc = (core + dc) % CORES
                    act(
                        k * chunk + pz * CORES + pc,
                        k * chunk + self_pos,
                        (pz * XS + px) * CORES + pc,
                    )

    def wait_bytes(ref, sem):
        pltpu.make_async_copy(ref, ref, sem).wait()

    def remote(src, dst, send_sem, recv_sem, device):
        return pltpu.make_async_remote_copy(
            src_ref=src,
            dst_ref=dst,
            send_sem=send_sems.at[send_sem],
            recv_sem=recv_sems.at[recv_sem],
            device_id=device,
            device_id_type=MESH,
        )

    get_tok = pltpu.make_async_copy(tok_hbm, tok, load_sems.at[0])
    get_idx = pltpu.make_async_copy(idx_hbm, idx, load_sems.at[1])
    get_kvw = pltpu.make_async_copy(kvw_hbm, kvw, load_sems.at[2])
    get_down = pltpu.make_async_copy(down_hbm, down, load_sems.at[3])
    get_idx.start()
    get_tok.start()

    barrier = pltpu.get_barrier_semaphore()

    for dz in Z_AWAY:
        for d in range(XS * CORES):
            if (dz, d) != (0, 0):
                to = (z + dz) % ZS * (XS * CORES) + (me + d) % (XS * CORES)
                pl.semaphore_signal(barrier, inc=1, device_id=(to, t), device_id_type=MESH)
    for d in Y_AWAY:
        pl.semaphore_signal(barrier, inc=1, device_id=(me, (t + d) % tensors), device_id_type=MESH)

    get_down.start()
    get_kvw.start()

    get_idx.wait()
    ids = idx[...]
    px = (ids >> 2) & 3
    offset = ((x + px) & 1) + 2 * (((x // 2) + (px >> 1)) & 1)
    place = offset * chunk_adapters + (ids >> 4) * (CORES * per_holder) + (ids & 3)
    places = lax.broadcasted_iota(jnp.int32, (adapters, rows), 0)
    picked = (places == place).astype(F32)
    earlier = lax.broadcasted_iota(jnp.int32, (rows, rows), 0) < lax.broadcasted_iota(
        jnp.int32, (rows, rows), 1
    )
    ordinal = jnp.dot(
        picked.astype(BF16), earlier.astype(F32).astype(BF16), preferred_element_type=F32
    )
    for m in range(MOST):
        chosen = jnp.where(ordinal == float(m), picked, 0.0)
        fsel[:, m * chunk_adapters : (m + 1) * chunk_adapters, :] = chosen.reshape(
            CHUNKS, chunk_adapters, rows
        )

    def gather_chunk(k):
        gathered = jnp.dot(fsel[k].astype(BF16), tok[...], preferred_element_type=F32)
        for m in range(MOST):
            of_m = gathered[m * chunk_adapters : (m + 1) * chunk_adapters]
            for j in range(blocks):
                stage[m, pl.ds(j, chunk_adapters, stride=blocks), :] = of_m[
                    :, j * LANES : (j + 1) * LANES
                ]
            send[k * chunk : (k + 1) * chunk, :, m * LANES : (m + 1) * LANES] = (
                stage[m, pl.ds(0, chunk * tile), :].reshape(chunk, tile, LANES).astype(BF16)
            )

    get_tok.wait()
    gather_chunk(0)

    pl.semaphore_wait(barrier, tensors - 1 + holders - 1)

    def dispatch_chunk(k):
        for_peers(
            k,
            (1, 0),
            lambda at, there, to: remote(
                send.at[at], recv.at[there], S_TOK, R_TOK + k, (to, t)
            ).start(),
        )

    dispatch_chunk(0)
    recv[self_pos] = send[self_pos]

    up[...] = jnp.zeros_like(up)
    get_ups = []
    for a in range(per_holder):
        rank = upq_hbm.shape[1]
        get_ups.append(
            pltpu.make_async_copy(
                upq_hbm.at[a], up.at[a, pl.ds(0, rank), pl.ds(0, features)], load_sems.at[4 + a]
            )
        )
        get_ups.append(
            pltpu.make_async_copy(
                upv_hbm.at[a],
                up.at[a, pl.ds(rank, rank), pl.ds(features, LANES)],
                load_sems.at[4 + per_holder + a],
            )
        )
    for copy in get_ups:
        copy.start()
    for c in range(2):
        spread = (
            lax.broadcasted_iota(jnp.int32, (LANES, 2 * LANES), 1)
            == 2 * lax.broadcasted_iota(jnp.int32, (LANES, 2 * LANES), 0) + c
        ).astype(F32).astype(BF16)
        for j in range(blocks):
            lhs[c, :, 2 * j * LANES : 2 * (j + 1) * LANES] = jnp.dot(
                tok[:, j * LANES : (j + 1) * LANES], spread, preferred_element_type=F32
            ).astype(BF16)
    gather_chunk(1)
    dispatch_chunk(1)
    get_kvw.wait()
    run = 32

    @pl.loop(0, features // run)
    def _(i):
        wbase[pl.ds(i * 2 * run, 2 * run), :] = kvw[pl.ds(i * run, run)].reshape(
            2 * run, wbase.shape[1]
        )

    gather_chunk(2)
    dispatch_chunk(2)
    @pl.loop(0, tensors // 2)
    def _(n):
        columns = pl.ds(pl.multiple_of(n * 2 * LANES, 2 * LANES), 2 * LANES)
        for c in range(2):
            terms = jnp.dot(lhs[c], wbase[:, columns], preferred_element_type=F32).astype(BF16)
            for half in range(2):
                bs_send[2 * n + half, :, c * LANES : (c + 1) * LANES] = terms[
                    :, half * LANES : (half + 1) * LANES
                ]

    gather_chunk(3)
    dispatch_chunk(3)

    def base_sends(ds):
        for d in ds:
            other = (t + d) % tensors
            remote(bs_send.at[other], bs_recv.at[t], S_BASE, R_BASE, (me, other)).start()

    base_sends(BASE_TO[0])
    bs_recv[t] = bs_send[t]
    ustage[MOST] = jnp.zeros_like(ustage[MOST])
    for k in range(CHUNKS):
        fturn[k] = fsel[k].T.astype(BF16)
    pairs = adapters // (CORES * per_holder)
    turned = (places == (place & 3) * pairs + (place >> 2)).astype(F32)
    turned_ordinal = jnp.dot(
        turned.astype(BF16), earlier.astype(F32).astype(BF16), preferred_element_type=F32
    )
    for m in range(MOST):
        chosen = jnp.where(turned_ordinal == float(m), turned, 0.0)
        vsel[:, m * adapters : (m + 1) * adapters] = chosen.T.astype(BF16)
    get_down.wait()
    for copy in get_ups:
        copy.wait()

    def arrive(k):
        wait_bytes(recv.at[pl.ds(0, chunk - 1 if k == 0 else chunk)], recv_sems.at[R_TOK + k])
        for m in range(MOST):
            stage[m, pl.ds(0, chunk * tile), :] = (
                recv[pl.ds(k * chunk, chunk), :, m * LANES : (m + 1) * LANES]
                .astype(F32)
                .reshape(chunk * tile, LANES)
            )
        for a in range(per_holder):
            for m in range(MOST):
                for j in range(blocks):
                    xs[a, m * chunk : (m + 1) * chunk, j * LANES : (j + 1) * LANES] = stage[
                        m, pl.ds(a * blocks + j, chunk, stride=tile), :
                    ].astype(BF16)
            terms = jnp.dot(xs[a], down[a], preferred_element_type=F32)
            for m in range(MOST):
                part[k, a * MOST + m] = terms[m * chunk : (m + 1) * chunk]

        for d in Y_AWAY:
            other = (t + d) % tensors

            @pl.when(other < owners)
            def _():
                remote(part.at[k, other], rs.at[k, t], S_SUM, R_SUM + k, (me, other)).start()

    def total(k):
        @pl.when(t < owners)
        def _():
            rs[k, t] = part[k, t]
            wait_bytes(rs.at[k, pl.ds(0, tensors - 1)], recv_sems.at[R_SUM + k])
            summed = rs[k, 0]
            for s in range(1, tensors):
                summed = summed + rs[k, s]
            sh[k, t] = summed.astype(BF16)

            for d in Y_AWAY:
                other = (t + d) % tensors
                remote(sh.at[k, t], sh.at[k, t], S_SHRUNK, R_SHRUNK + k, (me, other)).start()

    def corrections(k):
        @pl.when(t < owners)
        def _():
            wait_bytes(sh.at[k, pl.ds(0, owners - 1)], recv_sems.at[R_SHRUNK + k])

        @pl.when(t >= owners)
        def _():
            wait_bytes(sh.at[k, pl.ds(0, owners)], recv_sems.at[R_SHRUNK + k])

        for a in range(per_holder):
            shrunk = sh[k, a * MOST : (a + 1) * MOST].reshape(MOST * chunk, LANES)
            deltas = jnp.dot(shrunk, up[a], preferred_element_type=F32)
            for m in range(MOST):
                of_m = deltas[m * chunk : (m + 1) * chunk]
                for j in range(blocks):
                    ustage[m, pl.ds(a * blocks + j, chunk, stride=tile), :] = of_m[
                        :, j * LANES : (j + 1) * LANES
                    ]
                ustage[
                    MOST, pl.ds(a * blocks + m + core * (blocks // 2), chunk, stride=tile), :
                ] = of_m[:, features:]
        v_all[k] = ustage[MOST].reshape(ZS, CORES, tile, LANES).astype(BF16)
        remote(
            v_all.at[k, :, 1 - core], v_pair.at[k], S_PAIR, R_PAIR + k, (sibling, t)
        ).start()
        for m in range(MOST):
            ret_send[pl.ds(k * chunk, chunk), :, m * LANES : (m + 1) * LANES] = (
                ustage[m].reshape(chunk, tile, LANES).astype(BF16)
            )
        for_peers(
            k,
            (1, 0),
            lambda at, there, to: remote(
                ret_send.at[at], ret_recv.at[there], S_RET, R_RET + k, (to, t)
            ).start(),
        )
        if k == 0:
            ret_recv[self_pos] = ret_send[self_pos]

    def value_tiles(k):
        wait_bytes(v_pair.at[k], recv_sems.at[R_PAIR + k])
        v_send[k] = v_all[k, :, core] + v_pair[k]

        for_peers(
            k,
            (0,),
            lambda at, there, to: remote(
                v_send.at[k, at // CORES - k * ZS], v_recv.at[there // CORES], S_V, R_V, (to, t)
            ).start(),
        )
        if k == 0:
            v_recv[z] = v_send[k, z]

    def base_sum():
        wait_bytes(bs_recv.at[pl.ds(0, tensors - 1)], recv_sems.at[R_BASE])
        base = bs_recv[0].astype(F32)
        for s in range(1, tensors):
            base = base + bs_recv[s].astype(F32)
        k_out[...] = base[:, :LANES].astype(BF16)
        return base[:, LANES:]

    def select_back(k):
        wait_bytes(
            ret_recv.at[pl.ds(0, chunk - 1 if k == 0 else chunk)], recv_sems.at[R_RET + k]
        )
        for m in range(MOST):
            stage[m, pl.ds(0, chunk * tile), :] = (
                ret_recv[pl.ds(k * chunk, chunk), :, m * LANES : (m + 1) * LANES]
                .astype(F32)
                .reshape(chunk * tile, LANES)
            )
            for j in range(blocks):
                ys[
                    m * chunk_adapters : (m + 1) * chunk_adapters, j * LANES : (j + 1) * LANES
                ] = stage[m, pl.ds(j, chunk_adapters, stride=blocks), :].astype(BF16)
        found = jnp.dot(fturn[k], ys[...], preferred_element_type=F32)
        if k == 0:
            q_sum[...] = found
        elif k < CHUNKS - 1:
            q_sum[...] += found
        else:
            q_out[...] = (q_sum[...] + found).astype(BF16)

    def add_values(base_values):
        wait_bytes(v_recv.at[pl.ds(0, pairs - 1)], recv_sems.at[R_V])
        stage[0, pl.ds(0, pairs * tile), :] = v_recv[...].astype(F32).reshape(pairs * tile, LANES)
        gathered = jnp.concatenate(
            [
                stage[0, pl.ds(a * blocks + c * (blocks // 2) + m, pairs, stride=tile), :]
                for m in range(MOST)
                for c in range(CORES)
                for a in range(per_holder)
            ],
            axis=0,
        ).astype(BF16)
        v_out[...] = (
            base_values + jnp.dot(vsel[...], gathered, preferred_element_type=F32)
        ).astype(BF16)

    base_values = None
    for name in STEPS:
        if name == "base":
            base_values = base_sum()
        elif name == "values":
            add_values(base_values)
        else:
            of = {
                "a": arrive,
                "b": total,
                "c": corrections,
                "v": value_tiles,
                "f": select_back,
                "s": lambda k: base_sends(BASE_TO[k]),
            }
            of[name[0]](int(name[1]))

    wait_bytes(send.at[pl.ds(0, holders - 1)], send_sems.at[S_TOK])
    wait_bytes(bs_send.at[pl.ds(0, tensors - 1)], send_sems.at[S_BASE])

    @pl.when(t < owners)
    def _():
        for k in range(CHUNKS):
            wait_bytes(part.at[k, pl.ds(0, owners - 1)], send_sems.at[S_SUM])
            wait_bytes(
                rs.at[k, pl.ds(0, tensors - 1), pl.ds(0, chunk // 2)], send_sems.at[S_SHRUNK]
            )

    @pl.when(t >= owners)
    def _():
        for k in range(CHUNKS):
            wait_bytes(part.at[k, pl.ds(0, owners)], send_sems.at[S_SUM])

    wait_bytes(ret_send.at[pl.ds(0, holders - 1)], send_sems.at[S_RET])
    wait_bytes(v_pair, send_sems.at[S_PAIR])
    wait_bytes(v_recv.at[pl.ds(0, pairs - 1)], send_sems.at[S_V])


def step(holders, tensors, tokens, index, kv_weight, down, up_query, up_value):
    rows, features = tokens.shape
    head = kv_weight.shape[2] // tensors
    per_holder = down.shape[0]
    blocks = features // LANES
    tile = per_holder * blocks
    chunk = holders // CHUNKS
    owners = MOST * per_holder
    adapters = holders * per_holder
    pairs = holders // CORES
    vmem = pltpu.VMEM
    dma = pltpu.SemaphoreType.DMA
    scratch = [
        vmem(tokens.shape, BF16),
        vmem((1, rows), jnp.int32),
        vmem(kv_weight.shape, BF16),
        vmem((2 * features, kv_weight.shape[2]), BF16),
        vmem((2, rows, 2 * features), BF16),
        vmem(down.shape, BF16),
        vmem((per_holder, 2 * up_query.shape[1], features + LANES), BF16),
        vmem((CHUNKS, MOST * chunk * per_holder, rows), F32),
        vmem((CHUNKS, rows, MOST * chunk * per_holder), BF16),
        vmem((rows, MOST * adapters), BF16),
        vmem((MOST, holders * tile, LANES), F32),
        vmem((holders, tile, MOST * LANES), BF16),
        vmem((holders, tile, MOST * LANES), BF16),
        vmem((per_holder, MOST * chunk, features), BF16),
        vmem((CHUNKS, owners, chunk, LANES), F32),
        vmem((CHUNKS, tensors, chunk, LANES), F32),
        vmem((CHUNKS, owners, chunk, LANES), BF16),
        vmem((MOST + 1, chunk * tile, LANES), F32),
        vmem((holders, tile, MOST * LANES), BF16),
        vmem((holders, tile, MOST * LANES), BF16),
        vmem((MOST * chunk * per_holder, features), BF16),
        vmem((rows, features), F32),
        vmem((CHUNKS, ZS, CORES, tile, LANES), BF16),
        vmem((CHUNKS, ZS, tile, LANES), BF16),
        vmem((CHUNKS, ZS, tile, LANES), BF16),
        vmem((pairs, tile, LANES), BF16),
        vmem((tensors, rows, 2 * head), BF16),
        vmem((tensors, rows, 2 * head), BF16),
        dma((4 + 2 * per_holder,)),
        dma((7,)),
        dma((R_TOK + 5 * CHUNKS,)),
    ]
    return pl.pallas_call(
        functools.partial(kernel, holders, tensors),
        out_shape=(
            vmem((rows, features), BF16),
            vmem((rows, head), BF16),
            vmem((rows, head), BF16),
        ),
        in_specs=[pl.BlockSpec(memory_space=pltpu.HBM)] * 6,
        out_specs=tuple([pl.BlockSpec(memory_space=vmem)] * 3),
        scratch_shapes=scratch,
        compiler_params=pltpu.CompilerParams(
            collective_id=0, has_side_effects=True, vmem_limit_bytes=24 << 20
        ),
        name="adapters",
    )(
        *[
            pltpu.with_memory_space_constraint(operand, pltpu.HBM)
            for operand in (tokens, index.reshape(1, rows), kv_weight, down, up_query, up_value)
        ]
    )


def hand_over(*refs):
    count = len(refs) // 2
    copies = [
        pltpu.make_async_copy(refs[i], refs[count + i], refs[-1].at[i]) for i in range(count)
    ]
    for copy in copies:
        copy.start()
    for copy in copies:
        copy.wait()


def local(holders, tensors, *operands):
    outs = step(holders, tensors, *operands)
    return pl.pallas_call(
        hand_over,
        out_shape=tuple(jax.ShapeDtypeStruct(o.shape, o.dtype) for o in outs),
        in_specs=[pl.BlockSpec(memory_space=pltpu.VMEM)] * len(outs),
        out_specs=tuple([pl.BlockSpec(memory_space=pltpu.HBM)] * len(outs)),
        scratch_shapes=[pltpu.SemaphoreType.DMA((len(outs),))],
        compiler_params=pltpu.CompilerParams(vmem_limit_bytes=2 << 20),
        name="hand_over",
    )(*outs)


def solution(mesh):
    placed = (
        P("adapter", "tensor"),
        P("adapter", None),
        P("tensor", None, None),
        P("adapter", "tensor", None),
        P("adapter", None, "tensor"),
        P("adapter", None, "tensor"),
    )
    return jax.shard_map(
        functools.partial(local, mesh.shape["adapter"], mesh.shape["tensor"]),
        mesh=mesh,
        in_specs=placed,
        out_specs=(P("adapter", "tensor"), P("adapter", "tensor"), P("adapter", "tensor")),
        check_vma=False,
    )
```

```python
import functools
import jax
import jax.numpy as jnp
from jax import lax
from jax.experimental import pallas as pl
from jax.experimental.pallas import tpu as pltpu
from jax.sharding import PartitionSpec as P

MESH = pl.DeviceIdType.MESH
LANES = 128
BF16 = jnp.bfloat16
F32 = jnp.float32
MOST = 3
ZS, XS, CORES = 8, 4, 2
CHUNKS = XS
Z_AWAY = (4, 3, 5, 2, 6, 1, 7, 0)
Y_AWAY = (4, 3, 5, 2, 6, 1, 7)
STEPS = (
    "a0", "b0", "a1", "c0", "b1", "a2", "a3", "b2", "c1", "b3", "c2", "s1", "v0", "v1", "c3",
    "w2", "w3", "f0", "f1", "f2", "base", "values", "f3",
)
LATE = (2, 3)
BASE_TO = ((1, 7), (2, 6, 3, 5, 4))
R_BASE, R_V, R_TOK = 0, 1, 2
R_SUM, R_SHRUNK, R_RET, R_PAIR = (R_TOK + i * CHUNKS for i in range(1, 5))
S_TOK, S_BASE, S_SUM, S_SHRUNK, S_RET, S_PAIR, S_V = range(7)


def kernel(
    holders,
    tensors,
    tok_hbm,
    idx_hbm,
    kvw_hbm,
    down_hbm,
    upq_hbm,
    upv_hbm,
    q_out,
    k_out,
    v_out,
    tok,
    idx,
    kvw,
    wbase,
    lhs,
    down,
    up,
    fsel,
    fturn,
    vsel,
    stage,
    send,
    recv,
    xs,
    part,
    rs,
    sh,
    ustage,
    ret_send,
    ret_recv,
    ys,
    q_sum,
    v_all,
    v_pair,
    v_send,
    v_recv,
    bs_send,
    bs_recv,
    load_sems,
    send_sems,
    recv_sems,
):
    me = lax.axis_index("adapter")
    t = lax.axis_index("tensor")
    rows, features = tok.shape
    blocks = features // LANES
    per_holder = down.shape[0]
    adapters = holders * per_holder
    tile = per_holder * blocks
    chunk = holders // CHUNKS
    chunk_adapters = chunk * per_holder
    owners = MOST * per_holder
    z = me // (XS * CORES)
    x = (me // CORES) % XS
    core = me % CORES
    sibling = me + 1 - 2 * core
    self_pos = z * CORES + core

    def for_peers(k, cores, act):
        px = (x + k % 2 * (1 - 2 * (x % 2)) + 2 * (k // 2)) % XS
        for dz in Z_AWAY:
            pz = (z + dz) % ZS
            for dc in cores:
                if (k, dz, dc) != (0, 0, 0):
                    pc = (core + dc) % CORES
                    act(
                        k * chunk + pz * CORES + pc,
                        k * chunk + self_pos,
                        (pz * XS + px) * CORES + pc,
                    )

    def wait_bytes(ref, sem):
        pltpu.make_async_copy(ref, ref, sem).wait()

    def remote(src, dst, send_sem, recv_sem, device):
        return pltpu.make_async_remote_copy(
            src_ref=src,
            dst_ref=dst,
            send_sem=send_sems.at[send_sem],
            recv_sem=recv_sems.at[recv_sem],
            device_id=device,
            device_id_type=MESH,
        )

    get_tok = pltpu.make_async_copy(tok_hbm, tok, load_sems.at[0])
    get_idx = pltpu.make_async_copy(idx_hbm, idx, load_sems.at[1])
    get_kvw = pltpu.make_async_copy(kvw_hbm, kvw, load_sems.at[2])
    get_down = pltpu.make_async_copy(down_hbm, down, load_sems.at[3])
    get_idx.start()
    get_tok.start()

    barrier = pltpu.get_barrier_semaphore()

    for dz in Z_AWAY:
        for d in range(XS * CORES):
            if (dz, d) != (0, 0):
                to = (z + dz) % ZS * (XS * CORES) + (me + d) % (XS * CORES)
                pl.semaphore_signal(barrier, inc=1, device_id=(to, t), device_id_type=MESH)
    for d in Y_AWAY:
        pl.semaphore_signal(barrier, inc=1, device_id=(me, (t + d) % tensors), device_id_type=MESH)

    get_down.start()
    get_kvw.start()

    get_idx.wait()
    ids = idx[...]
    px = (ids >> 2) & 3
    offset = ((x + px) & 1) + 2 * (((x // 2) + (px >> 1)) & 1)
    place = offset * chunk_adapters + (ids >> 4) * (CORES * per_holder) + (ids & 3)
    places = lax.broadcasted_iota(jnp.int32, (adapters, rows), 0)
    picked = (places == place).astype(F32)
    earlier = lax.broadcasted_iota(jnp.int32, (rows, rows), 0) < lax.broadcasted_iota(
        jnp.int32, (rows, rows), 1
    )
    ordinal = jnp.dot(
        picked.astype(BF16), earlier.astype(F32).astype(BF16), preferred_element_type=F32
    )
    for m in range(MOST):
        chosen = jnp.where(ordinal == float(m), picked, 0.0)
        fsel[:, m * chunk_adapters : (m + 1) * chunk_adapters, :] = chosen.reshape(
            CHUNKS, chunk_adapters, rows
        )

    def gather_chunk(k):
        gathered = jnp.dot(fsel[k].astype(BF16), tok[...], preferred_element_type=F32)
        for m in range(MOST):
            of_m = gathered[m * chunk_adapters : (m + 1) * chunk_adapters]
            for j in range(blocks):
                stage[m, pl.ds(j, chunk_adapters, stride=blocks), :] = of_m[
                    :, j * LANES : (j + 1) * LANES
                ]
            send[k * chunk : (k + 1) * chunk, :, m * LANES : (m + 1) * LANES] = (
                stage[m, pl.ds(0, chunk * tile), :].reshape(chunk, tile, LANES).astype(BF16)
            )

    get_tok.wait()
    gather_chunk(0)

    pl.semaphore_wait(barrier, tensors - 1 + holders - 1)

    def dispatch_chunk(k):
        for_peers(
            k,
            (1, 0),
            lambda at, there, to: remote(
                send.at[at], recv.at[there], S_TOK, R_TOK + k, (to, t)
            ).start(),
        )

    dispatch_chunk(0)
    recv[self_pos] = send[self_pos]

    up[...] = jnp.zeros_like(up)
    get_ups = []
    for a in range(per_holder):
        rank = upq_hbm.shape[1]
        get_ups.append(
            pltpu.make_async_copy(
                upq_hbm.at[a], up.at[a, pl.ds(0, rank), pl.ds(0, features)], load_sems.at[4 + a]
            )
        )
        get_ups.append(
            pltpu.make_async_copy(
                upv_hbm.at[a],
                up.at[a, pl.ds(rank, rank), pl.ds(features, LANES)],
                load_sems.at[4 + per_holder + a],
            )
        )
    for copy in get_ups:
        copy.start()
    for c in range(2):
        spread = (
            lax.broadcasted_iota(jnp.int32, (LANES, 2 * LANES), 1)
            == 2 * lax.broadcasted_iota(jnp.int32, (LANES, 2 * LANES), 0) + c
        ).astype(F32).astype(BF16)
        for j in range(blocks):
            lhs[c, :, 2 * j * LANES : 2 * (j + 1) * LANES] = jnp.dot(
                tok[:, j * LANES : (j + 1) * LANES], spread, preferred_element_type=F32
            ).astype(BF16)
    gather_chunk(1)
    dispatch_chunk(1)
    get_kvw.wait()
    run = 32

    @pl.loop(0, features // run)
    def _(i):
        wbase[pl.ds(i * 2 * run, 2 * run), :] = kvw[pl.ds(i * run, run)].reshape(
            2 * run, wbase.shape[1]
        )

    gather_chunk(2)
    dispatch_chunk(2)
    @pl.loop(0, tensors // 2)
    def _(n):
        columns = pl.ds(pl.multiple_of(n * 2 * LANES, 2 * LANES), 2 * LANES)
        for c in range(2):
            terms = jnp.dot(lhs[c], wbase[:, columns], preferred_element_type=F32).astype(BF16)
            for half in range(2):
                bs_send[2 * n + half, :, c * LANES : (c + 1) * LANES] = terms[
                    :, half * LANES : (half + 1) * LANES
                ]

    gather_chunk(3)
    dispatch_chunk(3)

    def base_sends(ds):
        for d in ds:
            other = (t + d) % tensors
            remote(bs_send.at[other], bs_recv.at[t], S_BASE, R_BASE, (me, other)).start()

    base_sends(BASE_TO[0])
    bs_recv[t] = bs_send[t]
    ustage[MOST] = jnp.zeros_like(ustage[MOST])
    for k in range(CHUNKS):
        fturn[k] = fsel[k].T.astype(BF16)
    pairs = adapters // (CORES * per_holder)
    turned = (places == (place & 3) * pairs + (place >> 2)).astype(F32)
    turned_ordinal = jnp.dot(
        turned.astype(BF16), earlier.astype(F32).astype(BF16), preferred_element_type=F32
    )
    for m in range(MOST):
        chosen = jnp.where(turned_ordinal == float(m), turned, 0.0)
        vsel[:, m * adapters : (m + 1) * adapters] = chosen.T.astype(BF16)
    get_down.wait()
    for copy in get_ups:
        copy.wait()

    def arrive(k):
        wait_bytes(recv.at[pl.ds(0, chunk - 1 if k == 0 else chunk)], recv_sems.at[R_TOK + k])
        for m in range(MOST):
            stage[m, pl.ds(0, chunk * tile), :] = (
                recv[pl.ds(k * chunk, chunk), :, m * LANES : (m + 1) * LANES]
                .astype(F32)
                .reshape(chunk * tile, LANES)
            )
        for a in range(per_holder):
            for m in range(MOST):
                for j in range(blocks):
                    xs[a, m * chunk : (m + 1) * chunk, j * LANES : (j + 1) * LANES] = stage[
                        m, pl.ds(a * blocks + j, chunk, stride=tile), :
                    ].astype(BF16)
            terms = jnp.dot(xs[a], down[a], preferred_element_type=F32)
            for m in range(MOST):
                part[k, a * MOST + m] = terms[m * chunk : (m + 1) * chunk]

        for d in Y_AWAY:
            other = (t + d) % tensors

            @pl.when(other < owners)
            def _():
                remote(part.at[k, other], rs.at[k, t], S_SUM, R_SUM + k, (me, other)).start()

    def total(k):
        @pl.when(t < owners)
        def _():
            rs[k, t] = part[k, t]
            wait_bytes(rs.at[k, pl.ds(0, tensors - 1)], recv_sems.at[R_SUM + k])
            summed = rs[k, 0]
            for s in range(1, tensors):
                summed = summed + rs[k, s]
            sh[k, t] = summed.astype(BF16)

            for d in Y_AWAY:
                other = (t + d) % tensors
                remote(sh.at[k, t], sh.at[k, t], S_SHRUNK, R_SHRUNK + k, (me, other)).start()

    def corrections(k):
        @pl.when(t < owners)
        def _():
            wait_bytes(sh.at[k, pl.ds(0, owners - 1)], recv_sems.at[R_SHRUNK + k])

        @pl.when(t >= owners)
        def _():
            wait_bytes(sh.at[k, pl.ds(0, owners)], recv_sems.at[R_SHRUNK + k])

        for a in range(per_holder):
            shrunk = sh[k, a * MOST : (a + 1) * MOST].reshape(MOST * chunk, LANES)
            deltas = jnp.dot(shrunk, up[a], preferred_element_type=F32)
            for m in range(MOST):
                of_m = deltas[m * chunk : (m + 1) * chunk]
                for j in range(blocks):
                    ustage[m, pl.ds(a * blocks + j, chunk, stride=tile), :] = of_m[
                        :, j * LANES : (j + 1) * LANES
                    ]
                ustage[
                    MOST, pl.ds(a * blocks + m + core * (blocks // 2), chunk, stride=tile), :
                ] = of_m[:, features:]
        v_all[k] = ustage[MOST].reshape(ZS, CORES, tile, LANES).astype(BF16)
        remote(
            v_all.at[k, :, 1 - core], v_pair.at[k], S_PAIR, R_PAIR + k, (sibling, t)
        ).start()
        for m in range(MOST):
            ret_send[pl.ds(k * chunk, chunk), :, m * LANES : (m + 1) * LANES] = (
                ustage[m].reshape(chunk, tile, LANES).astype(BF16)
            )
        if k in LATE:
            pl.when(core == 0)(lambda: value_tiles(k))
        for_peers(
            k,
            (1, 0),
            lambda at, there, to: remote(
                ret_send.at[at], ret_recv.at[there], S_RET, R_RET + k, (to, t)
            ).start(),
        )
        if k == 0:
            ret_recv[self_pos] = ret_send[self_pos]

    def value_tiles(k):
        wait_bytes(v_pair.at[k], recv_sems.at[R_PAIR + k])
        v_send[k] = v_all[k, :, core] + v_pair[k]

        for_peers(
            k,
            (0,),
            lambda at, there, to: remote(
                v_send.at[k, at // CORES - k * ZS], v_recv.at[there // CORES], S_V, R_V, (to, t)
            ).start(),
        )
        if k == 0:
            v_recv[z] = v_send[k, z]

    def base_sum():
        wait_bytes(bs_recv.at[pl.ds(0, tensors - 1)], recv_sems.at[R_BASE])
        base = bs_recv[0].astype(F32)
        for s in range(1, tensors):
            base = base + bs_recv[s].astype(F32)
        k_out[...] = base[:, :LANES].astype(BF16)
        return base[:, LANES:]

    def select_back(k):
        wait_bytes(
            ret_recv.at[pl.ds(0, chunk - 1 if k == 0 else chunk)], recv_sems.at[R_RET + k]
        )
        for m in range(MOST):
            stage[m, pl.ds(0, chunk * tile), :] = (
                ret_recv[pl.ds(k * chunk, chunk), :, m * LANES : (m + 1) * LANES]
                .astype(F32)
                .reshape(chunk * tile, LANES)
            )
            for j in range(blocks):
                ys[
                    m * chunk_adapters : (m + 1) * chunk_adapters, j * LANES : (j + 1) * LANES
                ] = stage[m, pl.ds(j, chunk_adapters, stride=blocks), :].astype(BF16)
        found = jnp.dot(fturn[k], ys[...], preferred_element_type=F32)
        if k == 0:
            q_sum[...] = found
        elif k < CHUNKS - 1:
            q_sum[...] += found
        else:
            q_out[...] = (q_sum[...] + found).astype(BF16)

    def add_values(base_values):
        wait_bytes(v_recv.at[pl.ds(0, pairs - 1)], recv_sems.at[R_V])
        stage[0, pl.ds(0, pairs * tile), :] = v_recv[...].astype(F32).reshape(pairs * tile, LANES)
        gathered = jnp.concatenate(
            [
                stage[0, pl.ds(a * blocks + c * (blocks // 2) + m, pairs, stride=tile), :]
                for m in range(MOST)
                for c in range(CORES)
                for a in range(per_holder)
            ],
            axis=0,
        ).astype(BF16)
        v_out[...] = (
            base_values + jnp.dot(vsel[...], gathered, preferred_element_type=F32)
        ).astype(BF16)

    base_values = None
    for name in STEPS:
        if name == "base":
            base_values = base_sum()
        elif name == "values":
            add_values(base_values)
        else:
            of = {
                "a": arrive,
                "b": total,
                "c": corrections,
                "v": value_tiles,
                "w": lambda k: pl.when(core == 1)(lambda: value_tiles(k)),
                "f": select_back,
                "s": lambda k: base_sends(BASE_TO[k]),
            }
            of[name[0]](int(name[1]))

    wait_bytes(send.at[pl.ds(0, holders - 1)], send_sems.at[S_TOK])
    wait_bytes(bs_send.at[pl.ds(0, tensors - 1)], send_sems.at[S_BASE])

    @pl.when(t < owners)
    def _():
        for k in range(CHUNKS):
            wait_bytes(part.at[k, pl.ds(0, owners - 1)], send_sems.at[S_SUM])
            wait_bytes(
                rs.at[k, pl.ds(0, tensors - 1), pl.ds(0, chunk // 2)], send_sems.at[S_SHRUNK]
            )

    @pl.when(t >= owners)
    def _():
        for k in range(CHUNKS):
            wait_bytes(part.at[k, pl.ds(0, owners)], send_sems.at[S_SUM])

    wait_bytes(ret_send.at[pl.ds(0, holders - 1)], send_sems.at[S_RET])
    wait_bytes(v_pair, send_sems.at[S_PAIR])
    wait_bytes(v_recv.at[pl.ds(0, pairs - 1)], send_sems.at[S_V])


def step(holders, tensors, tokens, index, kv_weight, down, up_query, up_value):
    rows, features = tokens.shape
    head = kv_weight.shape[2] // tensors
    per_holder = down.shape[0]
    blocks = features // LANES
    tile = per_holder * blocks
    chunk = holders // CHUNKS
    owners = MOST * per_holder
    adapters = holders * per_holder
    pairs = holders // CORES
    vmem = pltpu.VMEM
    dma = pltpu.SemaphoreType.DMA
    scratch = [
        vmem(tokens.shape, BF16),
        vmem((1, rows), jnp.int32),
        vmem(kv_weight.shape, BF16),
        vmem((2 * features, kv_weight.shape[2]), BF16),
        vmem((2, rows, 2 * features), BF16),
        vmem(down.shape, BF16),
        vmem((per_holder, 2 * up_query.shape[1], features + LANES), BF16),
        vmem((CHUNKS, MOST * chunk * per_holder, rows), F32),
        vmem((CHUNKS, rows, MOST * chunk * per_holder), BF16),
        vmem((rows, MOST * adapters), BF16),
        vmem((MOST, holders * tile, LANES), F32),
        vmem((holders, tile, MOST * LANES), BF16),
        vmem((holders, tile, MOST * LANES), BF16),
        vmem((per_holder, MOST * chunk, features), BF16),
        vmem((CHUNKS, owners, chunk, LANES), F32),
        vmem((CHUNKS, tensors, chunk, LANES), F32),
        vmem((CHUNKS, owners, chunk, LANES), BF16),
        vmem((MOST + 1, chunk * tile, LANES), F32),
        vmem((holders, tile, MOST * LANES), BF16),
        vmem((holders, tile, MOST * LANES), BF16),
        vmem((MOST * chunk * per_holder, features), BF16),
        vmem((rows, features), F32),
        vmem((CHUNKS, ZS, CORES, tile, LANES), BF16),
        vmem((CHUNKS, ZS, tile, LANES), BF16),
        vmem((CHUNKS, ZS, tile, LANES), BF16),
        vmem((pairs, tile, LANES), BF16),
        vmem((tensors, rows, 2 * head), BF16),
        vmem((tensors, rows, 2 * head), BF16),
        dma((4 + 2 * per_holder,)),
        dma((7,)),
        dma((R_TOK + 5 * CHUNKS,)),
    ]
    return pl.pallas_call(
        functools.partial(kernel, holders, tensors),
        out_shape=(
            vmem((rows, features), BF16),
            vmem((rows, head), BF16),
            vmem((rows, head), BF16),
        ),
        in_specs=[pl.BlockSpec(memory_space=pltpu.HBM)] * 6,
        out_specs=tuple([pl.BlockSpec(memory_space=vmem)] * 3),
        scratch_shapes=scratch,
        compiler_params=pltpu.CompilerParams(
            collective_id=0, has_side_effects=True, vmem_limit_bytes=24 << 20
        ),
        name="adapters",
    )(
        *[
            pltpu.with_memory_space_constraint(operand, pltpu.HBM)
            for operand in (tokens, index.reshape(1, rows), kv_weight, down, up_query, up_value)
        ]
    )


def hand_over(*refs):
    count = len(refs) // 2
    copies = [
        pltpu.make_async_copy(refs[i], refs[count + i], refs[-1].at[i]) for i in range(count)
    ]
    for copy in copies:
        copy.start()
    for copy in copies:
        copy.wait()


def local(holders, tensors, *operands):
    outs = step(holders, tensors, *operands)
    return pl.pallas_call(
        hand_over,
        out_shape=tuple(jax.ShapeDtypeStruct(o.shape, o.dtype) for o in outs),
        in_specs=[pl.BlockSpec(memory_space=pltpu.VMEM)] * len(outs),
        out_specs=tuple([pl.BlockSpec(memory_space=pltpu.HBM)] * len(outs)),
        scratch_shapes=[pltpu.SemaphoreType.DMA((len(outs),))],
        compiler_params=pltpu.CompilerParams(vmem_limit_bytes=2 << 20),
        name="hand_over",
    )(*outs)


def solution(mesh):
    placed = (
        P("adapter", "tensor"),
        P("adapter", None),
        P("tensor", None, None),
        P("adapter", "tensor", None),
        P("adapter", None, "tensor"),
        P("adapter", None, "tensor"),
    )
    return jax.shard_map(
        functools.partial(local, mesh.shape["adapter"], mesh.shape["tensor"]),
        mesh=mesh,
        in_specs=placed,
        out_specs=(P("adapter", "tensor"), P("adapter", "tensor"), P("adapter", "tensor")),
        check_vma=False,
    )
```
